32 devices in a mesh: group: 2 (over x), dp: 4 (over y, core), mp: 4 (over z).
Axes of the slice: x: 2, y: 2, z: 4, core: 2. Of those that a mesh axis runs over, the one named last changes fastest.
Arguments:
- image_features: bfloat16 [1024, 6144], P('dp', 'mp'), may hold values from -6 to 6
- text_features: bfloat16 [1024, 1024], P('dp', 'mp'), may hold values from -6 to 6
- image_gain: float32 [6144], P('mp'), may hold values from 0.25 to 1.75
- text_gain: float32 [1024], P('mp'), may hold values from 0.25 to 1.75
- image_proj: bfloat16 [6144, 1024], P('mp'), may hold values from -1 to 1
- text_proj: bfloat16 [1024, 1024], P('mp'), may hold values from -1 to 1
- pair: int32 [1024], replicated, may hold values from 0 to 1023, each once
- logit_scale: float32 [], replicated, may hold values from 10 to 100
Outputs:
- embedding_grads: float32 [2, 1024, 1024], P('group', ('dp', 'mp'))
- loss: float32 [], replicated
The draws below stay inside these ranges and needn't reach their ends.
Inputs may be any that keep to these rules, and one draw needn't show every extreme that they name: `pair`: each caption belongs to exactly one image.
All inputs are finite; a program needn't handle non-finite values.
Results may differ from the reference program's by a relative error of at most 0.0061.
Values may be sent and summed in bfloat16 or wider, within the bound.
No kernel may reach another device: no remote copies, remote signals or barrier semaphores. Data moves between devices by JAX's collectives and lax.ppermute only.
A program may use at most 128 MiB of HBM per device.

```python
import jax
import jax.numpy as jnp
from jax import lax

D = 6144
DT = 1024
E = 1024
N = 1024


def caption_rows(key):
    base = jax.random.truncated_normal(jax.random.fold_in(key, 11), -6.0, 6.0, (N, DT), jnp.float32)
    return base


def caption_weights(key):
    values = jax.random.truncated_normal(jax.random.fold_in(key, 31), -4.0, 4.0, (DT, E), jnp.float32)
    return values * DT ** (-0.5)


def draw_text_features(key, part):
    return caption_rows(key).astype(jnp.bfloat16)


def draw_image_features(key, part):
    base = jax.random.truncated_normal(jax.random.fold_in(key, 21), -6.0, 6.0, (N, D), jnp.float32)
    return base.astype(jnp.bfloat16)


def draw_text_proj(key, part):
    return caption_weights(key).astype(jnp.bfloat16)


def draw_image_proj(key, part):
    values = jax.random.truncated_normal(jax.random.fold_in(key, 41), -4.0, 4.0, (D, E), jnp.float32) * D ** (-0.5)
    return values.astype(jnp.bfloat16)


def draw_logit_scale(key, part):
    return jax.random.uniform(key, (), jnp.float32, 10.0, 60.0)


def setup_inputs(seed: int = 0) -> dict:
    key_list = jax.random.split(jax.random.key(seed), 9)
    return {
        "image_features": draw_image_features(jax.random.fold_in(key_list[8], 71), 0),
        "text_features": draw_text_features(jax.random.fold_in(key_list[8], 71), 0),
        "image_gain": jnp.clip(1.0 + 0.15 * jax.random.normal(key_list[2], (D,), jnp.float32), 0.25, 1.75),
        "text_gain": jnp.clip(1.0 + 0.15 * jax.random.normal(key_list[3], (DT,), jnp.float32), 0.25, 1.75),
        "image_proj": draw_image_proj(jax.random.fold_in(key_list[8], 71), 0),
        "text_proj": draw_text_proj(jax.random.fold_in(key_list[8], 71), 0),
        "pair": jax.random.permutation(key_list[6], N).astype(jnp.int32),
        "logit_scale": draw_logit_scale(jax.random.fold_in(key_list[8], 71), 0),
    }


epsilon = 1e-05

def encode_tower(features, gain, projection):
    values = features.astype(jnp.float32)
    width = values.shape[1]
    average = lax.optimization_barrier(jnp.sum(values, axis=1)) / width
    spread = lax.optimization_barrier(jnp.sum(values * values, axis=1)) / width - average * average
    inverse = lax.rsqrt(spread + epsilon)
    normed = ((values - average[:, None]) * inverse[:, None] * gain[None, :]).astype(jnp.bfloat16)
    embedded = jnp.dot(normed, projection, preferred_element_type=jnp.float32)
    unit = embedded * lax.rsqrt(lax.optimization_barrier(jnp.sum(embedded * embedded, axis=1, keepdims=True)) + 1e-06)
    return unit.astype(jnp.bfloat16)

def row_totals(own, other, multiplier, span):
    blocks = own.reshape(-1, span, own.shape[1])

    def single(block):
        scores = multiplier * jnp.dot(block, other.T, preferred_element_type=jnp.float32)
        peak = lax.optimization_barrier(jnp.max(scores, axis=1))
        return peak + jnp.log(lax.optimization_barrier(jnp.sum(jnp.exp(scores - peak[:, None]), axis=1)))
    return lax.map(single, blocks).reshape(-1)

def side_grads(own, other, own_total, other_total, pair, multiplier, span, image_side):
    count_all = own.shape[0]
    starts = jnp.arange(count_all // span, dtype=jnp.int32) * span
    column_ids = jnp.arange(count_all, dtype=jnp.int32)

    def single(first):
        block = lax.dynamic_slice_in_dim(own, first, span, 0)
        totals = lax.dynamic_slice_in_dim(own_total, first, span, 0)
        scores = multiplier * jnp.dot(block, other.T, preferred_element_type=jnp.float32)
        row_ids = first + jnp.arange(span, dtype=jnp.int32)
        if image_side:
            matched = jnp.take(pair, row_ids)[:, None] == column_ids[None, :]
        else:
            matched = pair[None, :] == row_ids[:, None]
        flags = matched.astype(jnp.float32)
        target = jnp.sum(flags * scores)
        weights = multiplier * (jnp.exp(scores - totals[:, None]) + jnp.exp(scores - other_total[None, :]) - 2.0 * flags)
        grads = jnp.dot(weights.astype(jnp.bfloat16), other, preferred_element_type=jnp.float32)
        return (grads, target)
    grads, targets = lax.map(single, starts)
    return (grads.reshape(count_all, -1), jnp.sum(targets))

def reference(image_features, text_features, image_gain, text_gain, image_proj, text_proj, pair, logit_scale):
    image_unit = encode_tower(image_features, image_gain, image_proj)
    text_unit = encode_tower(text_features, text_gain, text_proj)
    count_all = image_unit.shape[0]
    span = min(512, count_all)
    image_total = row_totals(image_unit, text_unit, logit_scale, span)
    text_total = row_totals(text_unit, image_unit, logit_scale, span)
    image_grads, image_target = side_grads(image_unit, text_unit, image_total, text_total, pair, logit_scale, span, True)
    text_grads, text_target = side_grads(text_unit, image_unit, text_total, image_total, pair, logit_scale, span, False)
    loss = (jnp.sum(image_total) + jnp.sum(text_total) - image_target - text_target) / (2.0 * count_all)
    return (jnp.stack([image_grads, text_grads]), loss)
```

```python
import functools

import jax
import jax.numpy as jnp
from jax import lax
from jax.experimental import pallas as pl
from jax.experimental.pallas import tpu as pltpu
from jax.sharding import PartitionSpec as P

norm_epsilon = 1e-05
unit_epsilon = 1e-06
lanes = 128
VMEM = pl.BlockSpec(memory_space=pltpu.VMEM)
SMEM = pl.BlockSpec(memory_space=pltpu.SMEM)
ANY = pl.BlockSpec(memory_space=pl.ANY)
PARAMS = pltpu.CompilerParams(vmem_limit_bytes=48 * 1024 * 1024)


def exchange(shard, axis, distance):
    return lax.ppermute(shard, axis, [(i, i ^ distance) for i in range(lax.axis_size(axis))])


def cross_exchange(shard, distance):
    count = lax.axis_size("dp")
    pairs = [
        (side * count + i, (1 - side) * count + (i ^ distance))
        for side in range(2)
        for i in range(count)
    ]
    return lax.ppermute(shard, ("group", "dp"), pairs)


def tree(values, combine):
    values = list(values)
    while len(values) > 1:
        values = [combine(values[i], values[i + 1]) for i in range(0, len(values), 2)]
    return values[0]


def log_add(a, b):
    peak = jnp.maximum(a, b)
    return peak + jnp.log1p(jnp.exp(jnp.minimum(a, b) - peak))


def rows_to_lanes(columns):
    return jnp.transpose(columns)


def project_kernel(shards, info, image_x, text_x, image_g, text_g, image_p, text_p, *rest):
    own_out = rest[0]
    parts = rest[1:shards]
    notes = rest[shards : 2 * shards]
    x_buf, p_buf, total, stats, sems = rest[2 * shards :]
    rows = x_buf.shape[0]
    span = rows // shards
    width_out = total.shape[1]
    me = info[1]

    def tower(x_hbm, gain, p_hbm):
        width = x_hbm.shape[1]
        step = min(width, 512)
        chunks = width // step
        x_copy = pltpu.make_async_copy(x_hbm, x_buf.at[:, pl.ds(0, width)], sems.at[0])
        x_copy.start()
        copies = []
        for c in range(chunks):
            copy = pltpu.make_async_copy(
                p_hbm.at[pl.ds(c * step, step)], p_buf.at[pl.ds(c * step, step)], sems.at[1 + c]
            )
            copy.start()
            copies.append(copy)
        x_copy.wait()
        values = x_buf[:, :width].astype(jnp.float32)
        mean = jnp.sum(values, axis=1, keepdims=True) / width
        spread = jnp.sum((values - mean) * (values - mean), axis=1, keepdims=True)
        lane = lax.broadcasted_iota(jnp.int32, (rows, lanes), 1)
        stats[...] = jnp.where(lane == 0, mean, jnp.where(lane == 1, spread, 0.0))
        offset = jnp.zeros((16, width_out), jnp.float32)
        for c in range(chunks):
            g = gain[:, c * step : (c + 1) * step]
            high = g.astype(jnp.bfloat16).astype(jnp.float32)
            middle = (g - high).astype(jnp.bfloat16).astype(jnp.float32)
            low = g - high - middle
            row = lax.broadcasted_iota(jnp.int32, (16, step), 0)
            split = jnp.where(
                row == 0, high, jnp.where(row == 1, middle, jnp.where(row == 2, low, 0.0))
            ).astype(jnp.bfloat16)
            x = x_buf[:, c * step : (c + 1) * step].astype(jnp.float32)
            x = ((x - mean) * g).astype(jnp.bfloat16)
            copies[c].wait()
            p = p_buf[c * step : (c + 1) * step, :]
            product = jnp.dot(x, p, preferred_element_type=jnp.float32)
            if c == 0:
                total[...] = product
            else:
                total[...] += product
            offset += jnp.dot(split, p, preferred_element_type=jnp.float32)
        offset = jnp.sum(offset, axis=0, keepdims=True)
        height = width_out // lanes
        for k in range(shards):
            for j in range(height):
                notes[k][j : j + 1, :] = offset[:, j * lanes : (j + 1) * lanes]

    @pl.when(info[0] == 1)
    def _():
        tower(text_x, text_g, text_p)

    @pl.when(info[0] == 0)
    def _():
        tower(image_x, image_g, image_p)

    height = width_out // lanes
    for k in range(shards):
        first = pl.multiple_of((me ^ k) * span, span)
        block = total[pl.ds(first, span), :]
        if k == 0:
            own_out[...] = block
        else:
            parts[k - 1][...] = block.astype(jnp.bfloat16)
        one = stats[pl.ds(first, span), :]
        square = jnp.concatenate([one] * (lanes // span), axis=0)
        notes[k][height : height + 8, :] = rows_to_lanes(square)[:8, :]


def finish_kernel(shards, info, own, *rest):
    parts = rest[: shards - 1]
    notes = rest[shards - 1 : 2 * shards - 1]
    unit_out = rest[2 * shards - 1]
    span, width_out = own.shape
    height = width_out // lanes
    width = info[2].astype(jnp.float32)
    means, spreads = [], []
    for k in range(shards):
        stat = notes[k][height : height + 8, :]
        square = rows_to_lanes(jnp.concatenate([stat] * (lanes // 8), axis=0))[:span]
        means.append(square[:, 0:1])
        spreads.append(square[:, 1:2])
    mean = tree(means, jnp.add) / shards
    spread = tree(spreads, jnp.add) / width
    spread += tree([(m - mean) * (m - mean) for m in means], jnp.add) / shards
    inverse = lax.rsqrt(spread + norm_epsilon)
    pieces = []
    squares = jnp.zeros((span, lanes), jnp.float32)
    for j in range(height):
        at = slice(j * lanes, (j + 1) * lanes)
        value = own[:, at]
        for part in parts:
            value += part[:, at].astype(jnp.float32)
        for k in range(shards):
            value += (means[k] - mean) * notes[k][j : j + 1, :]
        value *= inverse
        squares += value * value
        pieces.append(value)
    scale = lax.rsqrt(jnp.sum(squares, axis=1, keepdims=True) + unit_epsilon)
    for j in range(height):
        unit_out[:, j * lanes : (j + 1) * lanes] = (pieces[j] * scale).astype(jnp.bfloat16)


def scores_kernel(owners, shards, info, multiplier, left, right, *rest):
    owns = rest[:owners]
    others = rest[owners : owners + shards]
    scores_out, row_out, column_out, gathered, mine = rest[owners + shards :]
    span = owns[0].shape[0]
    for k in range(shards):
        gathered[pl.ds(pl.multiple_of((info[1] ^ k) * span, span), span), :] = others[k][...]
    for k in range(owners):
        mine[pl.ds(pl.multiple_of((info[0] ^ k) * span, span), span), :] = owns[k][...]
    scores = multiplier[0] * lax.dot_general(
        mine[...], gathered[...], (((1,), (1,)), ((), ())), preferred_element_type=jnp.float32
    )
    scores_out[...] = scores
    row_peak = jnp.max(scores, axis=1, keepdims=True)
    row_part = row_peak + jnp.log(jnp.sum(jnp.exp(scores - row_peak), axis=1, keepdims=True))
    matched = left[...] == right[...]
    target = jnp.sum(jnp.where(matched, scores, 0.0), axis=1, keepdims=True)
    lane = lax.broadcasted_iota(jnp.int32, (scores.shape[0], lanes), 1)
    packed = jnp.where(lane == 0, row_part, jnp.where(lane == 1, target, 0.0))
    row_out[...] = rows_to_lanes(packed)[:8, :]
    column_peak = jnp.max(scores, axis=0, keepdims=True)
    column_out[...] = column_peak + jnp.log(
        jnp.sum(jnp.exp(scores - column_peak), axis=0, keepdims=True)
    )


def grads_kernel(owners, shards, info, multiplier, left, right, scores, gathered, *rest):
    row_parts = rest[:owners]
    column_parts = rest[owners : owners + shards]
    own_out, *outs, loss_out, total = rest[owners + shards :]
    span = own_out.shape[0]
    row_total = tree([r[0:1, :] for r in row_parts], log_add)
    target = tree([r[1:2, :] for r in row_parts], jnp.add)
    column_total = tree([c[...] for c in column_parts], log_add)
    loss = jnp.sum(row_total - target, axis=1, keepdims=True)
    loss_out[...] = jnp.broadcast_to(loss, loss_out.shape)
    row_total = jnp.transpose(jnp.broadcast_to(row_total, (lanes, row_total.shape[1])))[:, 0:1]
    matched = left[...] == right[...]
    values = scores[...]
    weights = multiplier[0] * (
        jnp.exp(values - row_total)
        + jnp.exp(values - column_total)
        - jnp.where(matched, 2.0, 0.0)
    )
    total[...] = jnp.dot(
        weights.astype(jnp.bfloat16), gathered[...], preferred_element_type=jnp.float32
    )
    for k in range(owners):
        first = pl.multiple_of((info[0] ^ k) * span, span)
        block = total[pl.ds(first, span), :]
        if k == 0:
            own_out[...] = block
        else:
            outs[k - 1][...] = block.astype(jnp.bfloat16)


def sum_kernel(own, *rest):
    value = own[...]
    for part in rest[:-1]:
        value += part[...].astype(jnp.float32)
    rest[-1][...] = value


def body(
    image_features, text_features, image_gain, text_gain, image_proj, text_proj, pair, logit_scale
):
    rows = image_features.shape[0]
    shards = lax.axis_size("mp")
    owners = lax.axis_size("dp")
    span = rows // shards
    width_out = image_proj.shape[1]
    group = lax.axis_index("group")
    me = lax.axis_index("mp")
    owner = lax.axis_index("dp")
    height = width_out // lanes + 8
    f32 = jnp.float32
    shape = jax.ShapeDtypeStruct

    text_side = group == 0
    widest = max(image_features.shape[1], text_features.shape[1])
    width = jnp.where(text_side, text_features.shape[1], image_features.shape[1]) * shards
    info = jnp.stack([text_side.astype(jnp.int32), me, width.astype(jnp.int32)])
    outs = pl.pallas_call(
        functools.partial(project_kernel, shards),
        out_shape=[shape((span, width_out), f32)]
        + [shape((span, width_out), jnp.bfloat16)] * (shards - 1)
        + [shape((height, lanes), f32)] * shards,
        in_specs=[SMEM, ANY, ANY, VMEM, VMEM, ANY, ANY],
        out_specs=[VMEM] * (2 * shards),
        scratch_shapes=[
            pltpu.VMEM((rows, widest), jnp.bfloat16),
            pltpu.VMEM((widest, width_out), jnp.bfloat16),
            pltpu.VMEM((rows, width_out), f32),
            pltpu.VMEM((rows, lanes), f32),
            pltpu.SemaphoreType.DMA((1 + max(1, widest // 512),)),
        ],
        compiler_params=PARAMS,
        name="project",
    )(
        info,
        image_features,
        text_features,
        image_gain[None, :],
        text_gain[None, :],
        image_proj,
        text_proj,
    )
    own, parts, notes = outs[0], outs[1:shards], outs[shards:]
    order = sorted(range(1, shards), key=lambda k: -k)
    parts = {k: exchange(parts[k - 1], "mp", k) for k in order}
    notes = [notes[0]] + [exchange(notes[k], "mp", k) for k in range(1, shards)]
    unit = pl.pallas_call(
        functools.partial(finish_kernel, shards),
        out_shape=shape((span, width_out), jnp.bfloat16),
        in_specs=[SMEM] + [VMEM] * (2 * shards),
        out_specs=VMEM,
        compiler_params=PARAMS,
        name="finish",
    )(info, own, *[parts[k] for k in range(1, shards)], *notes)

    others = [unit] + [exchange(unit, "mp", k) for k in range(1, shards)]
    owns = [cross_exchange(unit, k) for k in range(owners)]

    blocks = pair.reshape(owners, shards, span)
    row_count, column_count = owners * span, shards * span
    numbers = jnp.arange(owners * rows, dtype=jnp.int32).reshape(owners, shards, span)
    image_rows = group == 0
    row_pairs = lax.dynamic_slice_in_dim(blocks, me, 1, 1).reshape(row_count, 1)
    row_ids = lax.dynamic_slice_in_dim(numbers, me, 1, 1).reshape(row_count, 1)
    column_pairs = lax.dynamic_slice_in_dim(pair, owner * column_count, column_count, 0)[None, :]
    column_ids = owner * column_count + jnp.arange(column_count, dtype=jnp.int32)[None, :]
    left = jnp.where(image_rows, row_pairs, row_ids)
    right = jnp.where(image_rows, column_ids, column_pairs)
    place = jnp.stack([owner, me]).astype(jnp.int32)
    multiplier = logit_scale.reshape(1)

    scores, row_part, column_part, gathered = pl.pallas_call(
        functools.partial(scores_kernel, owners, shards),
        out_shape=[
            shape((row_count, column_count), f32),
            shape((8, row_count), f32),
            shape((1, column_count), f32),
            shape((column_count, width_out), jnp.bfloat16),
        ],
        in_specs=[SMEM, SMEM] + [VMEM] * (2 + owners + shards),
        out_specs=[VMEM] * 4,
        scratch_shapes=[pltpu.VMEM((row_count, width_out), jnp.bfloat16)],
        compiler_params=PARAMS,
        name="scores",
    )(place, multiplier, left, right, *owns, *others)
    row_parts = [row_part] + [exchange(row_part, "dp", k) for k in range(1, owners)]
    column_parts = [column_part] + [exchange(column_part, "mp", k) for k in range(1, shards)]

    own_grads, *grad_parts, loss = pl.pallas_call(
        functools.partial(grads_kernel, owners, shards),
        out_shape=[shape((span, width_out), f32)]
        + [shape((span, width_out), jnp.bfloat16)] * (owners - 1)
        + [shape((1, lanes), f32)],
        in_specs=[SMEM, SMEM] + [VMEM] * (4 + owners + shards),
        out_specs=[VMEM] * (owners + 1),
        scratch_shapes=[pltpu.VMEM((row_count, width_out), f32)],
        compiler_params=PARAMS,
        name="grads",
    )(place, multiplier, left, right, scores, gathered, *row_parts, *column_parts)
    grad_parts = [exchange(grad_parts[k - 1], "dp", k) for k in range(1, owners)]
    loss = loss + exchange(loss, "group", 1)
    distance = 1
    while distance < shards:
        loss = loss + exchange(loss, "mp", distance)
        distance *= 2
    loss = loss[0, 0] / (2.0 * owners * rows)
    grads = pl.pallas_call(
        sum_kernel,
        out_shape=shape((span, width_out), f32),
        in_specs=[VMEM] * owners,
        out_specs=VMEM,
        compiler_params=PARAMS,
        name="total",
    )(own_grads, *grad_parts)
    return (grads[None, :, :], loss)


def solution(mesh):
    in_specs = (
        P("dp", "mp"),
        P("dp", "mp"),
        P("mp"),
        P("mp"),
        P("mp", None),
        P("mp", None),
        P(),
        P(),
    )
    out_specs = (P("group", ("dp", "mp"), None), P())
    return jax.shard_map(body, mesh=mesh, in_specs=in_specs, out_specs=out_specs, check_vma=False)
```

```python
import functools

import jax
import jax.numpy as jnp
from jax import lax
from jax.experimental import pallas as pl
from jax.experimental.pallas import tpu as pltpu
from jax.sharding import PartitionSpec as P

norm_epsilon = 1e-05
unit_epsilon = 1e-06
lanes = 128
VMEM = pl.BlockSpec(memory_space=pltpu.VMEM)
SMEM = pl.BlockSpec(memory_space=pltpu.SMEM)
HBM = pl.BlockSpec(memory_space=pltpu.HBM)
PARAMS_P = pltpu.CompilerParams(vmem_limit_bytes=55500000)
PARAMS = pltpu.CompilerParams(vmem_limit_bytes=48 * 1024 * 1024)
f32 = jnp.float32
bf16 = jnp.bfloat16


def exchange(shard, axis, distance):
    return lax.ppermute(shard, axis, [(i, i ^ distance) for i in range(lax.axis_size(axis))])


def cross_exchange(shard, distance):
    count = lax.axis_size("mp")
    pairs = [
        (side * count + i, (1 - side) * count + (i ^ distance))
        for side in range(2)
        for i in range(count)
    ]
    return lax.ppermute(shard, ("group", "mp"), pairs)


def tree(values, combine):
    values = list(values)
    while len(values) > 1:
        values = [combine(values[i], values[i + 1]) for i in range(0, len(values), 2)]
    return values[0]


def log_add(a, b):
    peak = jnp.maximum(a, b)
    return peak + jnp.log1p(jnp.exp(jnp.minimum(a, b) - peak))


def merge_columns(a, b):
    row = lax.broadcasted_iota(jnp.int32, a.shape, 0)
    return jnp.where(row == 0, log_add(a, b), a + b)


def project_kernel(shards, image_x, text_x, image_g, text_g, image_p, text_p, *rest):
    own_out = rest[0]
    parts = rest[1:shards]
    note = rest[shards]
    x_buf, p_buf, total, sems = rest[shards + 1 :]
    rows = x_buf.shape[0]
    span = rows // shards
    width_out = total.shape[1]
    me = lax.axis_index("mp")

    def tower(x_hbm, gain, p_hbm):
        width = x_hbm.shape[1]
        step = min(width, 512)
        chunks = width // step
        x_copy = pltpu.make_async_copy(x_hbm, x_buf.at[:, pl.ds(0, width)], sems.at[0])
        x_copy.start()
        copies = []
        for c in range(chunks):
            copy = pltpu.make_async_copy(
                p_hbm.at[pl.ds(c * step, step)], p_buf.at[pl.ds(c * step, step)], sems.at[1 + c]
            )
            copy.start()
            copies.append(copy)
        x_copy.wait()
        values = x_buf[:, :width].astype(f32)
        mean = jnp.sum(values, axis=1, keepdims=True) / width
        spread = jnp.sum((values - mean) * (values - mean), axis=1, keepdims=True)
        lane = lax.broadcasted_iota(jnp.int32, (rows, lanes), 1)
        stats = jnp.transpose(jnp.where(lane == 0, mean, jnp.where(lane == 1, spread, 0.0)))
        offset = jnp.zeros((16, width_out), f32)
        for c in range(chunks):
            g = gain[c * step : (c + 1) * step].reshape(1, step)
            high = g.astype(bf16).astype(f32)
            middle = (g - high).astype(bf16).astype(f32)
            low = g - high - middle
            row = lax.broadcasted_iota(jnp.int32, (16, step), 0)
            split = jnp.where(
                row == 0, high, jnp.where(row == 1, middle, jnp.where(row == 2, low, 0.0))
            ).astype(bf16)
            x = x_buf[:, c * step : (c + 1) * step].astype(f32)
            x = ((x - mean) * g).astype(bf16)
            copies[c].wait()
            p = p_buf[c * step : (c + 1) * step, :]
            product = jnp.dot(x, p, preferred_element_type=f32)
            if c == 0:
                total[...] = product
            else:
                total[...] += product
            offset += jnp.dot(split, p, preferred_element_type=f32)
        offset = jnp.sum(offset, axis=0, keepdims=True)
        height = width_out // lanes
        for j in range(height):
            note[0, j : j + 1, :] = offset[:, j * lanes : (j + 1) * lanes]
        many = rows // lanes
        for j in range(many):
            for kind in range(2):
                at = height + kind * many + j
                note[0, at : at + 1, :] = stats[kind : kind + 1, j * lanes : (j + 1) * lanes]

    side = lax.axis_index("group")

    @pl.when(side == 0)
    def _():
        tower(text_x, text_g, text_p)

    @pl.when(side == 1)
    def _():
        tower(image_x, image_g, image_p)

    for k in range(shards):
        block = total[pl.ds(pl.multiple_of((me ^ k) * span, span), span), :]
        if k == 0:
            own_out[...] = block
        else:
            parts[k - 1][...] = block.astype(bf16)


def finish_kernel(shards, many, widths, own, *rest):
    parts = rest[: shards - 1]
    notes = rest[shards - 1 : -4]
    unit_out, turned = rest[-2:]
    span, width_out = own.shape
    height = width_out // lanes
    me = lax.axis_index("mp")
    width = jnp.where(lax.axis_index("group") == 0, widths[0], widths[1]).astype(f32)
    rows_of = []
    for n in notes:
        rows_of += [(n, i) for i in range(n.shape[0])]
    tail = notes[0].shape[1] - height
    stacked = [n[i, height:, :] for n, i in rows_of]
    stacked.append(jnp.zeros((-(-shards * tail // lanes) * lanes - shards * tail, lanes), f32))
    turned[...] = jnp.transpose(jnp.concatenate(stacked, axis=0))
    first = me * span
    block = turned[pl.ds(pl.multiple_of(lax.rem(first, lanes), span), span), :]
    lane = lax.broadcasted_iota(jnp.int32, block.shape, 1)
    pick = lax.div(first, lanes)

    def column(at):
        return jnp.sum(jnp.where(lane == at + pick, block, 0.0), axis=1, keepdims=True)

    means = [column(k * tail) for k in range(shards)]
    spreads = [column(k * tail + many) for k in range(shards)]
    mean = tree(means, jnp.add) / shards
    spread = tree(spreads, jnp.add) / width
    spread += tree([(m - mean) * (m - mean) for m in means], jnp.add) / shards
    inverse = lax.rsqrt(spread + norm_epsilon)
    pieces = []
    squares = jnp.zeros((span, lanes), f32)
    for j in range(height):
        at = slice(j * lanes, (j + 1) * lanes)
        value = own[:, at]
        for part in parts:
            value += part[:, at].astype(f32)
        for k, (n, i) in enumerate(rows_of):
            value += (means[k] - mean) * n[i, j : j + 1, :]
        value *= inverse
        squares += value * value
        pieces.append(value)
    scale = lax.rsqrt(jnp.sum(squares, axis=1, keepdims=True) + unit_epsilon)
    for j in range(height):
        unit_out[:, j * lanes : (j + 1) * lanes] = (pieces[j] * scale).astype(bf16)


def scores_kernel(halves, shards, multiplier, left, right, *rest):
    owns = rest[:4]
    others = rest[4:-5]
    scores_out, row_out, column_out, gathered, mine = rest[-5:]
    span = owns[0].shape[0]
    fars = shards // 2
    dp, mp = lax.axis_index("dp"), lax.axis_index("mp")
    core, near = lax.rem(dp, 2), lax.rem(mp, 2)
    half, far = lax.div(dp, 2), lax.div(mp, 2)
    for h in range(halves):
        for m in range(fars):
            at = ((half ^ h) * fars + (far ^ m)) * span
            gathered[pl.ds(pl.multiple_of(at, span), span), :] = others[h * fars + m][...]
    for c in range(2):
        for n in range(2):
            at = ((core ^ c) * 2 + (near ^ n)) * span
            mine[pl.ds(pl.multiple_of(at, span), span), :] = owns[c * 2 + n][...]
    scores = multiplier[0] * lax.dot_general(
        mine[...], gathered[...], (((1,), (1,)), ((), ())), preferred_element_type=f32
    )
    scores_out[...] = scores
    row_peak = jnp.max(scores, axis=1, keepdims=True)
    row_part = row_peak + jnp.log(jnp.sum(jnp.exp(scores - row_peak), axis=1, keepdims=True))
    row_out[...] = jnp.transpose(jnp.broadcast_to(row_part, (scores.shape[0], lanes)))[0:1, :]
    column_peak = jnp.max(scores, axis=0, keepdims=True)
    column_out[0:1, :] = column_peak + jnp.log(
        jnp.sum(jnp.exp(scores - column_peak), axis=0, keepdims=True)
    )
    matched = left[...] == right[...]
    column_out[1:2, :] = jnp.sum(jnp.where(matched, scores, 0.0), axis=0, keepdims=True)


def merge_kernel(row, row_other, column, column_other, row_out, column_out):
    row_out[...] = log_add(row[...], row_other[...])
    column_out[...] = merge_columns(column[...], column_other[...])


def grads_kernel(
    multiplier, left, right, scores, gathered, row, row_other, column, column_other, *rest
):
    kept_out, sent_out, loss_out, total = rest
    rows = kept_out.shape[0]
    core = lax.rem(lax.axis_index("dp"), 2)
    row_total = log_add(row[...], row_other[...])
    column_both = merge_columns(column[...], column_other[...])
    column_total = column_both[0:1, :]
    loss = jnp.sum(column_total - column_both[1:2, :], axis=1, keepdims=True)
    loss_out[...] = jnp.broadcast_to(loss, loss_out.shape)
    row_total = jnp.transpose(jnp.broadcast_to(row_total, (lanes, row_total.shape[1])))[:, 0:1]
    matched = left[...] == right[...]
    values = scores[...]
    weights = multiplier[0] * (
        jnp.exp(values - row_total)
        + jnp.exp(values - column_total)
        - jnp.where(matched, 2.0, 0.0)
    )
    total[...] = jnp.dot(weights.astype(bf16), gathered[...], preferred_element_type=f32)
    kept_out[...] = total[pl.ds(pl.multiple_of(core * rows, rows), rows), :]
    sent_out[...] = total[pl.ds(pl.multiple_of((1 - core) * rows, rows), rows), :].astype(bf16)


def halve_kernel(kept, received, loss, loss_other, own_out, sent_out, loss_out):
    rows = own_out.shape[0]
    near = lax.rem(lax.axis_index("mp"), 2)
    mine = pl.ds(pl.multiple_of(near * rows, rows), rows)
    yours = pl.ds(pl.multiple_of((1 - near) * rows, rows), rows)
    own_out[...] = kept[mine, :] + received[mine, :].astype(f32)
    sent_out[...] = (kept[yours, :] + received[yours, :].astype(f32)).astype(bf16)
    loss_out[...] = loss[...] + loss_other[...]


def total_kernel(scale, own, received, *rest):
    losses = rest[:4]
    out, loss_out = rest[4:]
    out[...] = own[...] + received[...].astype(f32)
    loss = tree([l[...] for l in losses], jnp.add)
    loss_out[...] = loss[:, 0:1] * scale


def body(
    image_features, text_features, image_gain, text_gain, image_proj, text_proj, pair, logit_scale
):
    rows = image_features.shape[0]
    shards = lax.axis_size("mp")
    owners = lax.axis_size("dp")
    halves, fars = owners // 2, shards // 2
    span = rows // shards
    width_out = image_proj.shape[1]
    group = lax.axis_index("group")
    me = lax.axis_index("mp")
    owner = lax.axis_index("dp")
    many = rows // lanes
    note_height = -(-(width_out // lanes + 2 * many) // 8) * 8
    shape = jax.ShapeDtypeStruct

    widest = max(image_features.shape[1], text_features.shape[1])
    own, *parts, note = pl.pallas_call(
        functools.partial(project_kernel, shards),
        out_shape=[shape((span, width_out), f32)]
        + [shape((span, width_out), bf16)] * (shards - 1)
        + [shape((1, note_height, lanes), f32)],
        in_specs=[HBM, HBM, VMEM, VMEM, HBM, HBM],
        out_specs=[VMEM] * (shards + 1),
        scratch_shapes=[
            pltpu.VMEM((rows, widest), bf16),
            pltpu.VMEM((widest, width_out), bf16),
            pltpu.VMEM((rows, width_out), f32),
            pltpu.SemaphoreType.DMA((1 + max(1, widest // 512),)),
        ],
        compiler_params=PARAMS_P,
        name="project",
    )(
        image_features,
        text_features,
        image_gain,
        text_gain,
        image_proj,
        text_proj,
    )
    parts = [exchange(parts[k - 1], "mp", k) for k in range(1, shards)]
    notes = [note]
    distance = 1
    while distance < shards:
        held = jnp.concatenate(notes, axis=0) if len(notes) > 1 else notes[0]
        notes.append(exchange(held, "mp", distance))
        distance *= 2

    core, near = owner % 2, me % 2
    half, far = owner // 2, me // 2
    numbers = jnp.arange(owners * rows, dtype=jnp.int32)
    cut = (halves, 2, fars, 2, span)

    def of_rows(v):
        return lax.dynamic_slice(
            v.reshape(cut), (half, 0, far, 0, 0), (1, 2, 1, 2, span)
        ).reshape(4 * span, 1)

    def of_columns(v):
        return lax.dynamic_slice(
            v.reshape(cut), (0, core, 0, near, 0), (halves, 1, fars, 1, span)
        ).reshape(1, halves * fars * span)

    image_rows = group == 0
    left = of_rows(jnp.where(image_rows, pair, numbers))
    right = of_columns(jnp.where(image_rows, numbers, pair))
    row_count, column_count = 4 * span, halves * fars * span
    multiplier = logit_scale.reshape(1)

    unit = pl.pallas_call(
        functools.partial(
            finish_kernel,
            shards,
            many,
            (text_features.shape[1] * shards, image_features.shape[1] * shards),
        ),
        out_shape=shape((span, width_out), bf16),
        in_specs=[VMEM] * (shards + len(notes) + 2),
        out_specs=VMEM,
        scratch_shapes=[
            pltpu.VMEM(
                (
                    lanes,
                    -(-shards * (note_height - width_out // lanes) // lanes) * lanes,
                ),
                f32,
            )
        ],
        compiler_params=PARAMS,
        name="finish",
    )(own, *parts, *notes, left, right)

    others = [unit] + [exchange(unit, "mp", m * 2) for m in range(1, fars)]
    mine = cross_exchange(unit, 0)
    owns = [mine, exchange(mine, "mp", 1)]
    blocks = list(others)
    for h in range(1, halves):
        blocks += [exchange(b, "dp", h * 2) for b in others]
    owns += [exchange(b, "dp", 1) for b in owns]

    scores, row_part, column_part, gathered = pl.pallas_call(
        functools.partial(scores_kernel, halves, shards),
        out_shape=[
            shape((row_count, column_count), f32),
            shape((1, row_count), f32),
            shape((2, column_count), f32),
            shape((column_count, width_out), bf16),
        ],
        in_specs=[SMEM] + [VMEM] * (2 + 4 + halves * fars),
        out_specs=[VMEM] * 4,
        scratch_shapes=[pltpu.VMEM((row_count, width_out), bf16)],
        compiler_params=PARAMS,
        name="scores",
    )(multiplier, left, right, *owns, *blocks)

    row_steps = [("dp", 1), ("mp", 1)]
    column_steps = [("dp", 2 << i) for i in range((halves - 1).bit_length())]
    column_steps += [("mp", 2 << i) for i in range((fars - 1).bit_length())]
    row, column = row_part, column_part
    while len(column_steps) > 2:
        axis, distance = column_steps.pop(0)
        column = merge_columns(column, exchange(column, axis, distance))
    for (row_axis, row_distance), (column_axis, column_distance) in zip(row_steps, column_steps):
        row_other = exchange(row, row_axis, row_distance)
        column_other = exchange(column, column_axis, column_distance)
        if row_axis == "dp":
            row, column = pl.pallas_call(
                merge_kernel,
                out_shape=[shape(row.shape, f32), shape(column.shape, f32)],
                in_specs=[VMEM] * 4,
                out_specs=[VMEM] * 2,
                compiler_params=PARAMS,
        name="merge",
            )(row, row_other, column, column_other)

    kept, sent, loss = pl.pallas_call(
        grads_kernel,
        out_shape=[
            shape((2 * span, width_out), f32),
            shape((2 * span, width_out), bf16),
            shape((1, lanes), f32),
        ],
        in_specs=[SMEM] + [VMEM] * 8,
        out_specs=[VMEM] * 3,
        scratch_shapes=[pltpu.VMEM((row_count, width_out), f32)],
        compiler_params=PARAMS,
        name="grads",
    )(multiplier, left, right, scores, gathered, row, row_other, column, column_other)
    own, sent, loss = pl.pallas_call(
        halve_kernel,
        out_shape=[
            shape((span, width_out), f32),
            shape((span, width_out), bf16),
            shape((1, lanes), f32),
        ],
        in_specs=[VMEM] * 4,
        out_specs=[VMEM] * 3,
        compiler_params=PARAMS,
        name="halve",
    )(kept, exchange(sent, "dp", 1), loss, exchange(loss, "dp", 1))
    grads, loss = pl.pallas_call(
        functools.partial(total_kernel, 1.0 / (2.0 * owners * rows)),
        out_shape=[shape((span, width_out), f32), shape((1, 1), f32)],
        in_specs=[VMEM] * 6,
        out_specs=[VMEM] * 2,
        compiler_params=PARAMS,
        name="total",
    )(
        own,
        exchange(sent, "mp", 1),
        loss,
        exchange(loss, "mp", 1),
        cross_exchange(loss, 0),
        cross_exchange(loss, 1),
    )
    return (grads[None, :, :], loss[0, 0])


def solution(mesh):
    in_specs = (
        P("dp", "mp"),
        P("dp", "mp"),
        P("mp"),
        P("mp"),
        P("mp", None),
        P("mp", None),
        P(),
        P(),
    )
    out_specs = (P("group", ("dp", "mp"), None), P())
    return jax.shard_map(body, mesh=mesh, in_specs=in_specs, out_specs=out_specs, check_vma=False)
```

```python
import functools

import jax
import jax.numpy as jnp
from jax import lax
from jax.experimental import pallas as pl
from jax.experimental.pallas import tpu as pltpu
from jax.sharding import PartitionSpec as P

norm_epsilon = 1e-05
unit_epsilon = 1e-06
lanes = 128
VMEM = pl.BlockSpec(memory_space=pltpu.VMEM)
SMEM = pl.BlockSpec(memory_space=pltpu.SMEM)
HBM = pl.BlockSpec(memory_space=pltpu.HBM)
PARAMS_P = pltpu.CompilerParams(vmem_limit_bytes=55500000)
PARAMS = pltpu.CompilerParams(vmem_limit_bytes=48 * 1024 * 1024)
f32 = jnp.float32
bf16 = jnp.bfloat16


def exchange(shard, axis, distance):
    return lax.ppermute(shard, axis, [(i, i ^ distance) for i in range(lax.axis_size(axis))])


def cross_exchange(shard, distance):
    count = lax.axis_size("mp")
    pairs = [
        (side * count + i, (1 - side) * count + (i ^ distance))
        for side in range(2)
        for i in range(count)
    ]
    return lax.ppermute(shard, ("group", "mp"), pairs)


def tree(values, combine):
    values = list(values)
    while len(values) > 1:
        values = [combine(values[i], values[i + 1]) for i in range(0, len(values), 2)]
    return values[0]


def log_add(a, b):
    peak = jnp.maximum(a, b)
    return peak + jnp.log1p(jnp.exp(jnp.minimum(a, b) - peak))


def merge_columns(a, b):
    row = lax.broadcasted_iota(jnp.int32, a.shape, 0)
    return jnp.where(row == 0, log_add(a, b), a + b)


def project_kernel(shards, image_x, text_x, image_g, text_g, image_p, text_p, *rest):
    own_out, kept_out, near_out, far_out, note, x_buf, p_buf, total, sems = rest
    rows = x_buf.shape[0]
    span = rows // shards
    width_out = total.shape[1]
    me = lax.axis_index("mp")

    def tower(x_hbm, gain, p_hbm):
        width = x_hbm.shape[1]
        step = min(width, 512)
        chunks = width // step
        x_copy = pltpu.make_async_copy(x_hbm, x_buf.at[:, pl.ds(0, width)], sems.at[0])
        x_copy.start()
        copies = []
        for c in range(chunks):
            copy = pltpu.make_async_copy(
                p_hbm.at[pl.ds(c * step, step)], p_buf.at[pl.ds(c * step, step)], sems.at[1 + c]
            )
            copy.start()
            copies.append(copy)
        x_copy.wait()
        values = x_buf[:, :width].astype(f32)
        mean = jnp.sum(values, axis=1, keepdims=True) / width
        spread = jnp.sum((values - mean) * (values - mean), axis=1, keepdims=True)
        lane = lax.broadcasted_iota(jnp.int32, (rows, lanes), 1)
        stats = jnp.transpose(jnp.where(lane == 0, mean, jnp.where(lane == 1, spread, 0.0)))
        offset = jnp.zeros((16, width_out), f32)
        for c in range(chunks):
            g = gain[c * step : (c + 1) * step].reshape(1, step)
            high = g.astype(bf16).astype(f32)
            middle = (g - high).astype(bf16).astype(f32)
            low = g - high - middle
            row = lax.broadcasted_iota(jnp.int32, (16, step), 0)
            split = jnp.where(
                row == 0, high, jnp.where(row == 1, middle, jnp.where(row == 2, low, 0.0))
            ).astype(bf16)
            x = x_buf[:, c * step : (c + 1) * step].astype(f32)
            x = ((x - mean) * g).astype(bf16)
            copies[c].wait()
            p = p_buf[c * step : (c + 1) * step, :]
            product = jnp.dot(x, p, preferred_element_type=f32)
            if c == 0:
                total[...] = product
            else:
                total[...] += product
            offset += jnp.dot(split, p, preferred_element_type=f32)
        offset = jnp.sum(offset, axis=0, keepdims=True)
        height = width_out // lanes
        for j in range(height):
            note[0, j : j + 1, :] = offset[:, j * lanes : (j + 1) * lanes]
        many = rows // lanes
        for j in range(many):
            for kind in range(2):
                at = height + kind * many + j
                note[0, at : at + 1, :] = stats[kind : kind + 1, j * lanes : (j + 1) * lanes]

    side = lax.axis_index("group")

    @pl.when(side == 0)
    def _():
        tower(text_x, text_g, text_p)

    @pl.when(side == 1)
    def _():
        tower(image_x, image_g, image_p)

    def block(distance):
        return total[pl.ds(pl.multiple_of((me ^ distance) * span, span), span), :]

    for m in range(1, shards // 2):
        at = slice((m - 1) * span, m * span)
        far_out[at, :] = block(2 * m + 1).astype(bf16)
        kept_out[at, :] = block(2 * m)
    near_out[...] = block(1).astype(bf16)
    own_out[...] = block(0)


def pair_kernel(kept, received, near, note, note_other, *rest):
    *outs, near_out, notes = rest
    near_out[...] = near[...]
    span = outs[0].shape[0]
    for m, out in enumerate(outs):
        at = slice(m * span, (m + 1) * span)
        out[...] = (kept[at, :] + received[at, :].astype(f32)).astype(bf16)
    notes[0] = note[0]
    notes[1] = note_other[0]


def finish_kernel(shards, many, widths, own, *rest):
    fars = shards // 2
    parts = rest[:fars]
    notes = rest[fars:-4]
    unit_out, turned = rest[-2:]
    span, width_out = own.shape
    height = width_out // lanes
    me = lax.axis_index("mp")
    width = jnp.where(lax.axis_index("group") == 0, widths[0], widths[1]).astype(f32)
    rows_of = []
    for n in notes:
        rows_of += [(n, i) for i in range(n.shape[0])]
    tail = notes[0].shape[1] - height
    stacked = [n[i, height:, :] for n, i in rows_of]
    stacked.append(jnp.zeros((-(-shards * tail // lanes) * lanes - shards * tail, lanes), f32))
    turned[...] = jnp.transpose(jnp.concatenate(stacked, axis=0))
    first = me * span
    block = turned[pl.ds(pl.multiple_of(lax.rem(first, lanes), span), span), :]
    lane = lax.broadcasted_iota(jnp.int32, block.shape, 1)
    pick = lax.div(first, lanes)

    def column(at):
        return jnp.sum(jnp.where(lane == at + pick, block, 0.0), axis=1, keepdims=True)

    means = [column(k * tail) for k in range(shards)]
    spreads = [column(k * tail + many) for k in range(shards)]
    mean = tree(means, jnp.add) / shards
    spread = tree(spreads, jnp.add) / width
    spread += tree([(m - mean) * (m - mean) for m in means], jnp.add) / shards
    inverse = lax.rsqrt(spread + norm_epsilon)
    pieces = []
    squares = jnp.zeros((span, lanes), f32)
    for j in range(height):
        at = slice(j * lanes, (j + 1) * lanes)
        value = own[:, at]
        for part in parts:
            value += part[:, at].astype(f32)
        for k, (n, i) in enumerate(rows_of):
            value += (means[k] - mean) * n[i, j : j + 1, :]
        value *= inverse
        squares += value * value
        pieces.append(value)
    scale = lax.rsqrt(jnp.sum(squares, axis=1, keepdims=True) + unit_epsilon)
    for j in range(height):
        unit_out[:, j * lanes : (j + 1) * lanes] = (pieces[j] * scale).astype(bf16)


def scores_kernel(halves, shards, multiplier, left, right, *rest):
    owns = rest[:4]
    others = rest[4:-5]
    scores_out, row_out, column_out, gathered, mine = rest[-5:]
    span = owns[0].shape[0]
    fars = shards // 2
    dp, mp = lax.axis_index("dp"), lax.axis_index("mp")
    core, near = lax.rem(dp, 2), lax.rem(mp, 2)
    half, far = lax.div(dp, 2), lax.div(mp, 2)
    for h in range(halves):
        for m in range(fars):
            at = ((half ^ h) * fars + (far ^ m)) * span
            gathered[pl.ds(pl.multiple_of(at, span), span), :] = others[h * fars + m][...]
    for c in range(2):
        for n in range(2):
            at = ((core ^ c) * 2 + (near ^ n)) * span
            mine[pl.ds(pl.multiple_of(at, span), span), :] = owns[c * 2 + n][...]
    scores = multiplier[0] * lax.dot_general(
        mine[...], gathered[...], (((1,), (1,)), ((), ())), preferred_element_type=f32
    )
    scores_out[...] = scores
    row_peak = jnp.max(scores, axis=1, keepdims=True)
    row_part = row_peak + jnp.log(jnp.sum(jnp.exp(scores - row_peak), axis=1, keepdims=True))
    row_out[...] = jnp.transpose(jnp.broadcast_to(row_part, (scores.shape[0], lanes)))[0:1, :]
    column_peak = jnp.max(scores, axis=0, keepdims=True)
    column_out[0:1, :] = column_peak + jnp.log(
        jnp.sum(jnp.exp(scores - column_peak), axis=0, keepdims=True)
    )
    matched = left[...] == right[...]
    column_out[1:2, :] = jnp.sum(jnp.where(matched, scores, 0.0), axis=0, keepdims=True)


def merge_kernel(row, row_other, column, column_other, row_out, column_out):
    row_out[...] = log_add(row[...], row_other[...])
    column_out[...] = merge_columns(column[...], column_other[...])


def grads_kernel(
    multiplier, left, right, scores, gathered, row, row_other, column, column_other, *rest
):
    kept_out, sent_out, loss_out, total = rest
    rows = kept_out.shape[0]
    core = lax.rem(lax.axis_index("dp"), 2)
    row_total = log_add(row[...], row_other[...])
    column_both = merge_columns(column[...], column_other[...])
    column_total = column_both[0:1, :]
    loss = jnp.sum(column_total - column_both[1:2, :], axis=1, keepdims=True)
    loss_out[...] = jnp.broadcast_to(loss, loss_out.shape)
    row_total = jnp.transpose(jnp.broadcast_to(row_total, (lanes, row_total.shape[1])))[:, 0:1]
    matched = left[...] == right[...]
    values = scores[...]
    weights = multiplier[0] * (
        jnp.exp(values - row_total)
        + jnp.exp(values - column_total)
        - jnp.where(matched, 2.0, 0.0)
    )
    total[...] = jnp.dot(weights.astype(bf16), gathered[...], preferred_element_type=f32)
    kept_out[...] = total[pl.ds(pl.multiple_of(core * rows, rows), rows), :]
    sent_out[...] = total[pl.ds(pl.multiple_of((1 - core) * rows, rows), rows), :].astype(bf16)


def halve_kernel(kept, received, loss, loss_other, own_out, sent_out, loss_out):
    loss_out[...] = loss[...] + loss_other[...]
    rows = own_out.shape[0]
    near = lax.rem(lax.axis_index("mp"), 2)
    mine = pl.ds(pl.multiple_of(near * rows, rows), rows)
    yours = pl.ds(pl.multiple_of((1 - near) * rows, rows), rows)
    own_out[...] = kept[mine, :] + received[mine, :].astype(f32)
    sent_out[...] = (kept[yours, :] + received[yours, :].astype(f32)).astype(bf16)


def total_kernel(scale, own, received, *rest):
    losses = rest[:4]
    out, loss_out = rest[4:]
    out[...] = own[...] + received[...].astype(f32)
    loss = tree([l[...] for l in losses], jnp.add)
    loss_out[...] = loss[:, 0:1] * scale


def body(
    image_features, text_features, image_gain, text_gain, image_proj, text_proj, pair, logit_scale
):
    rows = image_features.shape[0]
    shards = lax.axis_size("mp")
    owners = lax.axis_size("dp")
    halves, fars = owners // 2, shards // 2
    span = rows // shards
    width_out = image_proj.shape[1]
    group = lax.axis_index("group")
    me = lax.axis_index("mp")
    owner = lax.axis_index("dp")
    many = rows // lanes
    note_height = -(-(width_out // lanes + 2 * many) // 8) * 8
    shape = jax.ShapeDtypeStruct

    widest = max(image_features.shape[1], text_features.shape[1])
    own, kept, near_part, far_part, note = pl.pallas_call(
        functools.partial(project_kernel, shards),
        out_shape=[
            shape((span, width_out), f32),
            shape(((fars - 1) * span, width_out), f32),
            shape((span, width_out), bf16),
            shape(((fars - 1) * span, width_out), bf16),
            shape((1, note_height, lanes), f32),
        ],
        in_specs=[HBM, HBM, VMEM, VMEM, HBM, HBM],
        out_specs=[VMEM] * 5,
        scratch_shapes=[
            pltpu.VMEM((rows, widest), bf16),
            pltpu.VMEM((widest, width_out), bf16),
            pltpu.VMEM((rows, width_out), f32),
            pltpu.SemaphoreType.DMA((1 + max(1, widest // 512),)),
        ],
        compiler_params=PARAMS_P,
        name="project",
    )(
        image_features,
        text_features,
        image_gain,
        text_gain,
        image_proj,
        text_proj,
    )
    far_other = exchange(far_part, "mp", 1)
    note_other = exchange(note, "mp", 1)
    *pairs, near_part, both = pl.pallas_call(
        pair_kernel,
        out_shape=[shape((span, width_out), bf16)] * fars
        + [shape((2, note_height, lanes), f32)],
        in_specs=[VMEM] * 5,
        out_specs=[VMEM] * (fars + 1),
        compiler_params=PARAMS,
        name="pair",
    )(kept, far_other, near_part, note, note_other)
    parts = []
    notes = [both]
    for m in range(1, fars):
        parts.append(exchange(pairs[m - 1], "mp", 2 * m))
        notes.append(exchange(both, "mp", 2 * m))
    parts.append(exchange(near_part, "mp", 1))

    core, near = owner % 2, me % 2
    half, far = owner // 2, me // 2
    numbers = jnp.arange(owners * rows, dtype=jnp.int32)
    cut = (halves, 2, fars, 2, span)

    def of_rows(v):
        return lax.dynamic_slice(
            v.reshape(cut), (half, 0, far, 0, 0), (1, 2, 1, 2, span)
        ).reshape(4 * span, 1)

    def of_columns(v):
        return lax.dynamic_slice(
            v.reshape(cut), (0, core, 0, near, 0), (halves, 1, fars, 1, span)
        ).reshape(1, halves * fars * span)

    image_rows = group == 0
    left = of_rows(jnp.where(image_rows, pair, numbers))
    right = of_columns(jnp.where(image_rows, numbers, pair))
    row_count, column_count = 4 * span, halves * fars * span
    multiplier = logit_scale.reshape(1)

    unit = pl.pallas_call(
        functools.partial(
            finish_kernel,
            shards,
            many,
            (text_features.shape[1] * shards, image_features.shape[1] * shards),
        ),
        out_shape=shape((span, width_out), bf16),
        in_specs=[VMEM] * (1 + len(parts) + len(notes) + 2),
        out_specs=VMEM,
        scratch_shapes=[
            pltpu.VMEM(
                (
                    lanes,
                    -(-shards * (note_height - width_out // lanes) // lanes) * lanes,
                ),
                f32,
            )
        ],
        compiler_params=PARAMS,
        name="finish",
    )(own, *parts, *notes, left, right)

    others = [unit] + [exchange(unit, "mp", m * 2) for m in range(1, fars)]
    owns = [cross_exchange(unit, 0), cross_exchange(unit, 1)]
    blocks = list(others)
    for h in range(1, halves):
        blocks += [exchange(b, "dp", h * 2) for b in others]
    owns += [exchange(b, "dp", 1) for b in owns]

    scores, row_part, column_part, gathered = pl.pallas_call(
        functools.partial(scores_kernel, halves, shards),
        out_shape=[
            shape((row_count, column_count), f32),
            shape((1, row_count), f32),
            shape((2, column_count), f32),
            shape((column_count, width_out), bf16),
        ],
        in_specs=[SMEM] + [VMEM] * (2 + 4 + halves * fars),
        out_specs=[VMEM] * 4,
        scratch_shapes=[pltpu.VMEM((row_count, width_out), bf16)],
        compiler_params=PARAMS,
        name="scores",
    )(multiplier, left, right, *owns, *blocks)

    row_steps = [("dp", 1), ("mp", 1)]
    column_steps = [("dp", 2 << i) for i in range((halves - 1).bit_length())]
    column_steps += [("mp", 2 << i) for i in range((fars - 1).bit_length())]
    row, column = row_part, column_part
    while len(column_steps) > 2:
        axis, distance = column_steps.pop(0)
        column = merge_columns(column, exchange(column, axis, distance))
    for (row_axis, row_distance), (column_axis, column_distance) in zip(row_steps, column_steps):
        row_other = exchange(row, row_axis, row_distance)
        column_other = exchange(column, column_axis, column_distance)
        if row_axis == "dp":
            row, column = pl.pallas_call(
                merge_kernel,
                out_shape=[shape(row.shape, f32), shape(column.shape, f32)],
                in_specs=[VMEM] * 4,
                out_specs=[VMEM] * 2,
                compiler_params=PARAMS,
        name="merge",
            )(row, row_other, column, column_other)

    kept, sent, loss = pl.pallas_call(
        grads_kernel,
        out_shape=[
            shape((2 * span, width_out), f32),
            shape((2 * span, width_out), bf16),
            shape((1, lanes), f32),
        ],
        in_specs=[SMEM] + [VMEM] * 8,
        out_specs=[VMEM] * 3,
        scratch_shapes=[pltpu.VMEM((row_count, width_out), f32)],
        compiler_params=PARAMS,
        name="grads",
    )(multiplier, left, right, scores, gathered, row, row_other, column, column_other)
    own, sent, loss = pl.pallas_call(
        halve_kernel,
        out_shape=[
            shape((span, width_out), f32),
            shape((span, width_out), bf16),
            shape((1, lanes), f32),
        ],
        in_specs=[VMEM] * 4,
        out_specs=[VMEM] * 3,
        compiler_params=PARAMS,
        name="halve",
    )(kept, exchange(sent, "dp", 1), loss, exchange(loss, "dp", 1))
    grads, loss = pl.pallas_call(
        functools.partial(total_kernel, 1.0 / (2.0 * owners * rows)),
        out_shape=[shape((span, width_out), f32), shape((1, 1), f32)],
        in_specs=[VMEM] * 6,
        out_specs=[VMEM] * 2,
        compiler_params=PARAMS,
        name="total",
    )(
        own,
        exchange(sent, "mp", 1),
        loss,
        exchange(loss, "mp", 1),
        cross_exchange(loss, 0),
        cross_exchange(loss, 1),
    )
    return (grads[None, :, :], loss[0, 0])


def solution(mesh):
    in_specs = (
        P("dp", "mp"),
        P("dp", "mp"),
        P("mp"),
        P("mp"),
        P("mp", None),
        P("mp", None),
        P(),
        P(),
    )
    out_specs = (P("group", ("dp", "mp"), None), P())
    return jax.shard_map(body, mesh=mesh, in_specs=in_specs, out_specs=out_specs, check_vma=False)
```

```python
import functools

import jax
import jax.numpy as jnp
from jax import lax
from jax.experimental import pallas as pl
from jax.experimental.pallas import tpu as pltpu
from jax.sharding import PartitionSpec as P

norm_epsilon = 1e-05
unit_epsilon = 1e-06
lanes = 128
X_CUTS = 1
R_BLOCK = 16
ROW_COPIES = 8
COLUMN_COPIES = 8
P_STEP = 512
VMEM = pl.BlockSpec(memory_space=pltpu.VMEM)
SMEM = pl.BlockSpec(memory_space=pltpu.SMEM)
HBM = pl.BlockSpec(memory_space=pltpu.HBM)
PARAMS_P = pltpu.CompilerParams(vmem_limit_bytes=55500000)
PARAMS = pltpu.CompilerParams(vmem_limit_bytes=48 * 1024 * 1024)
f32 = jnp.float32
bf16 = jnp.bfloat16


def exchange(shard, axis, distance):
    return lax.ppermute(shard, axis, [(i, i ^ distance) for i in range(lax.axis_size(axis))])


def cross_exchange(shard, distance):
    count = lax.axis_size("mp")
    pairs = [
        (side * count + i, (1 - side) * count + (i ^ distance))
        for side in range(2)
        for i in range(count)
    ]
    return lax.ppermute(shard, ("group", "mp"), pairs)


def tree(values, combine):
    values = list(values)
    while len(values) > 1:
        values = [combine(values[i], values[i + 1]) for i in range(0, len(values), 2)]
    return values[0]


def log_add(a, b):
    peak = jnp.maximum(a, b)
    return peak + jnp.log1p(jnp.exp(jnp.minimum(a, b) - peak))


def merge_columns(a, b):
    row = lax.broadcasted_iota(jnp.int32, a.shape, 0)
    return jnp.where(row == 0, log_add(a, b), a + b)


def split_rows(value, rows):
    high = value.astype(bf16).astype(f32)
    middle = (value - high).astype(bf16).astype(f32)
    low = value - high - middle
    row = lax.broadcasted_iota(jnp.int32, (rows, value.shape[1]), 0)
    parts = jnp.where(row == 0, high, jnp.where(row == 1, middle, jnp.where(row == 2, low, 0.0)))
    return parts.astype(bf16)


def project_kernel(shards, x_hbm, gain, p_hbm, *rest):
    own_out, kept_out, near_out, far_out, note, x_buf, p_buf, scaled, total, sems = rest
    rows, width = x_buf.shape
    span = rows // shards
    width_out = total.shape[1]
    me = lax.axis_index("mp")
    some = rows // X_CUTS
    x_copies = []
    for c in range(X_CUTS):
        at = pl.ds(c * some, some)
        copy = pltpu.make_async_copy(x_hbm.at[at], x_buf.at[at], sems.at[c])
        copy.start()
        x_copies.append(copy)
    cuts = max(1, width // P_STEP)
    deep = width // cuts
    copies = []
    for c in range(cuts):
        at = pl.ds(c * deep, deep)
        copy = pltpu.make_async_copy(p_hbm.at[at], p_buf.at[at], sems.at[X_CUTS + c])
        copy.start()
        copies.append(copy)
    g = gain[...].reshape(1, width)
    scaled[rows:, :] = split_rows(g, 16)
    packs = []
    lane = lax.broadcasted_iota(jnp.int32, (R_BLOCK, lanes), 1)
    for c in range(X_CUTS):
        x_copies[c].wait()
        for r in range(c * some, (c + 1) * some, R_BLOCK):
            at = slice(r, r + R_BLOCK)
            values = x_buf[at, :].astype(f32)
            mean = jnp.sum(values, axis=1, keepdims=True) / width
            centred = values - mean
            spread = jnp.sum(centred * centred, axis=1, keepdims=True)
            scaled[at, :] = (centred * g).astype(bf16)
            packs.append(jnp.where(lane == 0, mean, jnp.where(lane == 1, spread, 0.0)))
    stats = jnp.transpose(jnp.concatenate(packs, axis=0))
    height = width_out // lanes
    many = rows // lanes
    for j in range(many):
        for kind in range(2):
            at = height + kind * many + j
            note[0, at : at + 1, :] = stats[kind : kind + 1, j * lanes : (j + 1) * lanes]
    for c in range(cuts):
        copies[c].wait()
        at = slice(c * deep, (c + 1) * deep)
        product = jnp.dot(scaled[:, at], p_buf[at, :], preferred_element_type=f32)
        if c == 0:
            total[...] = product
        else:
            total[...] += product
    offset = jnp.sum(total[rows:, :], axis=0, keepdims=True)
    for j in range(height):
        note[0, j : j + 1, :] = offset[:, j * lanes : (j + 1) * lanes]

    def block(distance):
        return total[pl.ds(pl.multiple_of((me ^ distance) * span, span), span), :]

    for m in range(1, shards // 2):
        at = slice((m - 1) * span, m * span)
        far_out[at, :] = block(2 * m + 1).astype(bf16)
        kept_out[at, :] = block(2 * m)
    near_out[...] = block(1).astype(bf16)
    own_out[...] = block(0)


def pair_kernel(kept, received, near, *rest):
    *outs, near_out = rest
    near_out[...] = near[...]
    span = outs[0].shape[0]
    for m, out in enumerate(outs):
        at = slice(m * span, (m + 1) * span)
        out[...] = (kept[at, :] + received[at, :].astype(f32)).astype(bf16)


def both_kernel(note, note_other, notes):
    notes[0] = note[0]
    notes[1] = note_other[0]


def finish_kernel(shards, many, widths, own, *rest):
    fars = shards // 2
    parts = rest[:fars]
    notes = rest[fars:-4]
    unit_out, turned = rest[-2:]
    span, width_out = own.shape
    height = width_out // lanes
    me = lax.axis_index("mp")
    width = jnp.where(lax.axis_index("group") == 0, widths[0], widths[1]).astype(f32)
    rows_of = []
    for n in notes:
        rows_of += [(n, i) for i in range(n.shape[0])]
    tail = notes[0].shape[1] - height
    stacked = [n[i, height:, :] for n, i in rows_of]
    stacked.append(jnp.zeros((-(-shards * tail // lanes) * lanes - shards * tail, lanes), f32))
    turned[...] = jnp.transpose(jnp.concatenate(stacked, axis=0))
    first = me * span
    block = turned[pl.ds(pl.multiple_of(lax.rem(first, lanes), span), span), :]
    lane = lax.broadcasted_iota(jnp.int32, block.shape, 1)
    pick = lax.div(first, lanes)

    def column(at):
        return jnp.sum(jnp.where(lane == at + pick, block, 0.0), axis=1, keepdims=True)

    means = [column(k * tail) for k in range(shards)]
    spreads = [column(k * tail + many) for k in range(shards)]
    mean = tree(means, jnp.add) / shards
    spread = tree(spreads, jnp.add) / width
    spread += tree([(m - mean) * (m - mean) for m in means], jnp.add) / shards
    inverse = lax.rsqrt(spread + norm_epsilon)
    pieces = []
    squares = jnp.zeros((span, lanes), f32)
    for j in range(height):
        at = slice(j * lanes, (j + 1) * lanes)
        value = own[:, at]
        for part in parts:
            value += part[:, at].astype(f32)
        for k, (n, i) in enumerate(rows_of):
            value += (means[k] - mean) * n[i, j : j + 1, :]
        value *= inverse
        squares += value * value
        pieces.append(value)
    scale = lax.rsqrt(jnp.sum(squares, axis=1, keepdims=True) + unit_epsilon)
    for j in range(height):
        unit_out[:, j * lanes : (j + 1) * lanes] = (pieces[j] * scale).astype(bf16)


def scores_kernel(halves, shards, multiplier, left, right, *rest):
    owns = rest[:4]
    others = rest[4:-5]
    scores_out, row_out, column_out, gathered, mine = rest[-5:]
    span = owns[0].shape[0]
    fars = shards // 2
    dp, mp = lax.axis_index("dp"), lax.axis_index("mp")
    core, near = lax.rem(dp, 2), lax.rem(mp, 2)
    half, far = lax.div(dp, 2), lax.div(mp, 2)
    for h in range(halves):
        for m in range(fars):
            at = ((half ^ h) * fars + (far ^ m)) * span
            gathered[pl.ds(pl.multiple_of(at, span), span), :] = others[h * fars + m][...]
    for c in range(2):
        for n in range(2):
            at = ((core ^ c) * 2 + (near ^ n)) * span
            mine[pl.ds(pl.multiple_of(at, span), span), :] = owns[c * 2 + n][...]
    scores = multiplier[0] * lax.dot_general(
        mine[...], gathered[...], (((1,), (1,)), ((), ())), preferred_element_type=f32
    )
    scores_out[...] = scores
    row_peak = jnp.max(scores, axis=1, keepdims=True)
    row_part = row_peak + jnp.log(jnp.sum(jnp.exp(scores - row_peak), axis=1, keepdims=True))
    row_out[...] = jnp.transpose(jnp.broadcast_to(row_part, (scores.shape[0], lanes)))[0:1, :]
    column_peak = jnp.max(scores, axis=0, keepdims=True)
    column_part = column_peak + jnp.log(
        jnp.sum(jnp.exp(scores - column_peak), axis=0, keepdims=True)
    )
    matched = left[...] == right[...]
    target = jnp.sum(jnp.where(matched, scores, 0.0), axis=0, keepdims=True)
    row = lax.broadcasted_iota(jnp.int32, column_out.shape, 0)
    column_out[...] = jnp.where(row == 0, column_part, jnp.where(row == 1, target, 0.0))


def merge_rows_kernel(row, row_other, out):
    out[...] = jnp.broadcast_to(log_add(row[...], row_other[...]), out.shape)


def merge_columns_kernel(column, column_other, after, out):
    out[...] = merge_columns(column[0:2, :], column_other[0:2, :])


def grads_kernel(
    multiplier, left, right, scores, gathered, column, column_other, *rest
):
    row, row_other, kept_out, sent_out, loss_out, total = rest
    rows, width_out = kept_out.shape
    core = lax.rem(lax.axis_index("dp"), 2)
    row_total = log_add(row[0:1, :], row_other[0:1, :])
    column_both = merge_columns(column[...], column_other[...])
    column_total = column_both[0:1, :]
    loss = jnp.sum(column_total - column_both[1:2, :], axis=1, keepdims=True)
    loss = jnp.broadcast_to(loss, loss_out.shape)
    loss_out[...] = loss
    sent_out[:, width_out:] = split_rows(loss, rows)
    row_total = jnp.transpose(jnp.broadcast_to(row_total, (lanes, row_total.shape[1])))[:, 0:1]
    matched = left[...] == right[...]
    values = scores[...]
    weights = multiplier[0] * (
        jnp.exp(values - row_total)
        + jnp.exp(values - column_total)
        - jnp.where(matched, 2.0, 0.0)
    )
    total[...] = jnp.dot(weights.astype(bf16), gathered[...], preferred_element_type=f32)
    kept_out[...] = total[pl.ds(pl.multiple_of(core * rows, rows), rows), :]
    sent_out[:, :width_out] = total[
        pl.ds(pl.multiple_of((1 - core) * rows, rows), rows), :
    ].astype(bf16)


def halve_kernel(kept, received, loss, own_out, sent_out, loss_out):
    rows, width_out = own_out.shape
    near = lax.rem(lax.axis_index("mp"), 2)
    mine = pl.ds(pl.multiple_of(near * rows, rows), rows)
    yours = pl.ds(pl.multiple_of((1 - near) * rows, rows), rows)
    loss = loss[...] + jnp.sum(received[:, width_out:].astype(f32), axis=0, keepdims=True)
    loss_out[...] = loss
    own_out[...] = kept[mine, :] + received[mine, :width_out].astype(f32)
    sent_out[:, :width_out] = (kept[yours, :] + received[yours, :width_out].astype(f32)).astype(bf16)
    sent_out[:, width_out:] = split_rows(loss, rows)


def total_kernel(scale, own, received, loss, there, there_near, out, loss_out):
    width_out = own.shape[1]
    out[...] = own[...] + received[:, :width_out].astype(f32)
    near = jnp.sum(received[:, width_out:].astype(f32), axis=0, keepdims=True)
    loss = (loss[...] + near) + (there[...] + there_near[...])
    loss_out[...] = loss[:, 0:1] * scale


def body(
    image_features, text_features, image_gain, text_gain, image_proj, text_proj, pair, logit_scale
):
    rows = image_features.shape[0]
    shards = lax.axis_size("mp")
    owners = lax.axis_size("dp")
    halves, fars = owners // 2, shards // 2
    span = rows // shards
    width_out = image_proj.shape[1]
    group = lax.axis_index("group")
    me = lax.axis_index("mp")
    owner = lax.axis_index("dp")
    many = rows // lanes
    note_height = -(-(width_out // lanes + 2 * many) // 8) * 8
    shape = jax.ShapeDtypeStruct

    def project(x, gain, p):
        width = x.shape[1]
        return pl.pallas_call(
            functools.partial(project_kernel, shards),
            out_shape=[
                shape((span, width_out), f32),
                shape(((fars - 1) * span, width_out), f32),
                shape((span, width_out), bf16),
                shape(((fars - 1) * span, width_out), bf16),
                shape((1, note_height, lanes), f32),
            ],
            in_specs=[HBM, VMEM, HBM],
            out_specs=[VMEM] * 5,
            scratch_shapes=[
                pltpu.VMEM((rows, width), bf16),
                pltpu.VMEM((width, width_out), bf16),
                pltpu.VMEM((rows + 16, width), bf16),
                pltpu.VMEM((rows + 16, width_out), f32),
                pltpu.SemaphoreType.DMA((X_CUTS + max(1, width // P_STEP),)),
            ],
            compiler_params=PARAMS_P,
            name="project",
        )(x, gain, p)

    own, kept, near_part, far_part, note = lax.cond(
        group == 0,
        lambda: project(text_features, text_gain, text_proj),
        lambda: project(image_features, image_gain, image_proj),
    )
    far_other = exchange(far_part, "mp", 1)
    note_other = exchange(note, "mp", 1)
    *pairs, near_part = pl.pallas_call(
        pair_kernel,
        out_shape=[shape((span, width_out), bf16)] * fars,
        in_specs=[VMEM] * 3,
        out_specs=[VMEM] * fars,
        compiler_params=PARAMS,
        name="pair",
    )(kept, far_other, near_part)
    both = pl.pallas_call(
        both_kernel,
        out_shape=shape((2, note_height, lanes), f32),
        in_specs=[VMEM] * 2,
        out_specs=VMEM,
        compiler_params=PARAMS,
        name="both",
    )(note, note_other)
    parts = []
    notes = [both]
    for m in range(1, fars):
        parts.append(exchange(pairs[m - 1], "mp", 2 * m))
        notes.append(exchange(both, "mp", 2 * m))
    parts.append(exchange(near_part, "mp", 1))

    core, near = owner % 2, me % 2
    half, far = owner // 2, me // 2
    numbers = jnp.arange(owners * rows, dtype=jnp.int32)
    cut = (halves, 2, fars, 2, span)

    def of_rows(v):
        return lax.dynamic_slice(
            v.reshape(cut), (half, 0, far, 0, 0), (1, 2, 1, 2, span)
        ).reshape(4 * span, 1)

    def of_columns(v):
        return lax.dynamic_slice(
            v.reshape(cut), (0, core, 0, near, 0), (halves, 1, fars, 1, span)
        ).reshape(1, halves * fars * span)

    image_rows = group == 0
    left = of_rows(jnp.where(image_rows, pair, numbers))
    right = of_columns(jnp.where(image_rows, numbers, pair))
    row_count, column_count = 4 * span, halves * fars * span
    multiplier = logit_scale.reshape(1)

    unit = pl.pallas_call(
        functools.partial(
            finish_kernel,
            shards,
            many,
            (text_features.shape[1] * shards, image_features.shape[1] * shards),
        ),
        out_shape=shape((span, width_out), bf16),
        in_specs=[VMEM] * (1 + len(parts) + len(notes) + 2),
        out_specs=VMEM,
        scratch_shapes=[
            pltpu.VMEM(
                (
                    lanes,
                    -(-shards * (note_height - width_out // lanes) // lanes) * lanes,
                ),
                f32,
            )
        ],
        compiler_params=PARAMS,
        name="finish",
    )(own, *parts, *notes, left, right)

    others = [unit] + [exchange(unit, "mp", m * 2) for m in range(1, fars)]
    owns = [cross_exchange(unit, 0), cross_exchange(unit, 1)]
    blocks = list(others)
    for h in range(1, halves):
        blocks += [exchange(b, "dp", h * 2) for b in others]
    owns += [exchange(b, "dp", 1) for b in owns]

    scores, row_part, column_part, gathered = pl.pallas_call(
        functools.partial(scores_kernel, halves, shards),
        out_shape=[
            shape((row_count, column_count), f32),
            shape((1, row_count), f32),
            shape((COLUMN_COPIES, column_count), f32),
            shape((column_count, width_out), bf16),
        ],
        in_specs=[SMEM] + [VMEM] * (2 + 4 + halves * fars),
        out_specs=[VMEM] * 4,
        scratch_shapes=[pltpu.VMEM((row_count, width_out), bf16)],
        compiler_params=PARAMS,
        name="scores",
    )(multiplier, left, right, *owns, *blocks)

    def merged(kernel, height, *operands):
        return pl.pallas_call(
            kernel,
            out_shape=shape((height, operands[0].shape[1]), f32),
            in_specs=[VMEM] * len(operands),
            out_specs=VMEM,
            compiler_params=PARAMS,
            name="merge",
        )(*operands)

    column_steps = [("dp", 2 << i) for i in range((halves - 1).bit_length())]
    column_steps += [("mp", 2 << i) for i in range((fars - 1).bit_length())]
    row, column = row_part, column_part
    row = merged(merge_rows_kernel, ROW_COPIES, row, exchange(row, "dp", 1))
    row_other = exchange(row, "mp", 1)
    for axis, distance in column_steps[:-1]:
        column = merged(merge_columns_kernel, 2, column, exchange(column, axis, distance), row)
    column_other = exchange(column, *column_steps[-1])

    kept, sent, loss = pl.pallas_call(
        grads_kernel,
        out_shape=[
            shape((2 * span, width_out), f32),
            shape((2 * span, width_out + lanes), bf16),
            shape((1, lanes), f32),
        ],
        in_specs=[SMEM] + [VMEM] * 8,
        out_specs=[VMEM] * 3,
        scratch_shapes=[pltpu.VMEM((row_count, width_out), f32)],
        compiler_params=PARAMS,
        name="grads",
    )(multiplier, left, right, scores, gathered, column, column_other, row, row_other)
    own, sent, loss = pl.pallas_call(
        halve_kernel,
        out_shape=[
            shape((span, width_out), f32),
            shape((span, width_out + lanes), bf16),
            shape((1, lanes), f32),
        ],
        in_specs=[VMEM] * 3,
        out_specs=[VMEM] * 3,
        compiler_params=PARAMS,
        name="halve",
    )(kept, exchange(sent, "dp", 1), loss)
    there, there_near = cross_exchange(loss, 0), cross_exchange(loss, 1)
    grads, loss = pl.pallas_call(
        functools.partial(total_kernel, 1.0 / (2.0 * owners * rows)),
        out_shape=[shape((span, width_out), f32), shape((1, 1), f32)],
        in_specs=[VMEM] * 5,
        out_specs=[VMEM] * 2,
        compiler_params=PARAMS,
        name="total",
    )(own, exchange(sent, "mp", 1), loss, there, there_near)
    return (grads[None, :, :], loss[0, 0])


def solution(mesh):
    in_specs = (
        P("dp", "mp"),
        P("dp", "mp"),
        P("mp"),
        P("mp"),
        P("mp", None),
        P("mp", None),
        P(),
        P(),
    )
    out_specs = (P("group", ("dp", "mp"), None), P())
    return jax.shard_map(body, mesh=mesh, in_specs=in_specs, out_specs=out_specs, check_vma=False)
```

```python
import functools

import jax
import jax.numpy as jnp
from jax import lax
from jax.experimental import pallas as pl
from jax.experimental.pallas import tpu as pltpu
from jax.sharding import PartitionSpec as P

norm_epsilon = 1e-05
unit_epsilon = 1e-06
lanes = 128
X_CUTS = 1
R_BLOCK = 16
ROW_COPIES = 8
COLUMN_COPIES = 8
P_STEP = 512
VMEM = pl.BlockSpec(memory_space=pltpu.VMEM)
SMEM = pl.BlockSpec(memory_space=pltpu.SMEM)
HBM = pl.BlockSpec(memory_space=pltpu.HBM)
PARAMS_P = pltpu.CompilerParams(vmem_limit_bytes=55500000)
PARAMS = pltpu.CompilerParams(vmem_limit_bytes=48 * 1024 * 1024)
f32 = jnp.float32
bf16 = jnp.bfloat16


def exchange(shard, axis, distance):
    return lax.ppermute(shard, axis, [(i, i ^ distance) for i in range(lax.axis_size(axis))])


def cross_exchange(shard, distance):
    count = lax.axis_size("mp")
    pairs = [
        (side * count + i, (1 - side) * count + (i ^ distance))
        for side in range(2)
        for i in range(count)
    ]
    return lax.ppermute(shard, ("group", "mp"), pairs)


def tree(values, combine):
    values = list(values)
    while len(values) > 1:
        values = [combine(values[i], values[i + 1]) for i in range(0, len(values), 2)]
    return values[0]


def log_add(a, b):
    peak = jnp.maximum(a, b)
    return peak + jnp.log1p(jnp.exp(jnp.minimum(a, b) - peak))


def merge_columns(a, b):
    row = lax.broadcasted_iota(jnp.int32, a.shape, 0)
    return jnp.where(row == 0, log_add(a, b), a + b)


def split_rows(value, rows):
    high = value.astype(bf16).astype(f32)
    middle = (value - high).astype(bf16).astype(f32)
    low = value - high - middle
    row = lax.broadcasted_iota(jnp.int32, (rows, value.shape[1]), 0)
    parts = jnp.where(row == 0, high, jnp.where(row == 1, middle, jnp.where(row == 2, low, 0.0)))
    return parts.astype(bf16)


def project_kernel(shards, x_hbm, gain, p_hbm, *rest):
    own_out, kept_out, near_out, far_out, note, x_buf, p_buf, scaled, total, sems = rest
    rows, width = x_buf.shape
    span = rows // shards
    width_out = total.shape[1]
    me = lax.axis_index("mp")
    some = rows // X_CUTS
    x_copies = []
    for c in range(X_CUTS):
        at = pl.ds(c * some, some)
        copy = pltpu.make_async_copy(x_hbm.at[at], x_buf.at[at], sems.at[c])
        copy.start()
        x_copies.append(copy)
    cuts = max(1, width // P_STEP)
    deep = width // cuts
    copies = []
    for c in range(cuts):
        at = pl.ds(c * deep, deep)
        copy = pltpu.make_async_copy(p_hbm.at[at], p_buf.at[at], sems.at[X_CUTS + c])
        copy.start()
        copies.append(copy)
    g = gain[...].reshape(1, width)
    scaled[rows:, :] = split_rows(g, 16)
    packs = []
    lane = lax.broadcasted_iota(jnp.int32, (R_BLOCK, lanes), 1)
    for c in range(X_CUTS):
        x_copies[c].wait()
        for r in range(c * some, (c + 1) * some, R_BLOCK):
            at = slice(r, r + R_BLOCK)
            values = x_buf[at, :].astype(f32)
            mean = jnp.sum(values, axis=1, keepdims=True) / width
            centred = values - mean
            spread = jnp.sum(centred * centred, axis=1, keepdims=True)
            scaled[at, :] = (centred * g).astype(bf16)
            packs.append(jnp.where(lane == 0, mean, jnp.where(lane == 1, spread, 0.0)))
    stats = jnp.transpose(jnp.concatenate(packs, axis=0))
    height = width_out // lanes
    many = rows // lanes
    for j in range(many):
        for kind in range(2):
            at = height + kind * many + j
            note[0, at : at + 1, :] = stats[kind : kind + 1, j * lanes : (j + 1) * lanes]
    for c in range(cuts):
        copies[c].wait()
        at = slice(c * deep, (c + 1) * deep)
        product = jnp.dot(scaled[:, at], p_buf[at, :], preferred_element_type=f32)
        if c == 0:
            total[...] = product
        else:
            total[...] += product
    offset = jnp.sum(total[rows:, :], axis=0, keepdims=True)
    for j in range(height):
        note[0, j : j + 1, :] = offset[:, j * lanes : (j + 1) * lanes]

    def block(distance):
        return total[pl.ds(pl.multiple_of((me ^ distance) * span, span), span), :]

    for m in range(1, shards // 2):
        at = slice((m - 1) * span, m * span)
        far_out[at, :] = block(2 * m + 1).astype(bf16)
        kept_out[at, :] = block(2 * m)
    near_out[...] = block(1).astype(bf16)
    own_out[...] = block(0)


def pair_kernel(kept, received, near, *rest):
    *outs, near_out = rest
    near_out[...] = near[...]
    span = outs[0].shape[0]
    for m, out in enumerate(outs):
        at = slice(m * span, (m + 1) * span)
        out[...] = (kept[at, :] + received[at, :].astype(f32)).astype(bf16)


def both_kernel(note, note_other, notes):
    notes[0] = note[0]
    notes[1] = note_other[0]


def finish_kernel(shards, many, widths, own, *rest):
    fars = shards // 2
    parts = rest[:fars]
    notes = rest[fars:-4]
    unit_out, turned = rest[-2:]
    span, width_out = own.shape
    height = width_out // lanes
    me = lax.axis_index("mp")
    width = jnp.where(lax.axis_index("group") == 0, widths[0], widths[1]).astype(f32)
    rows_of = []
    for n in notes:
        rows_of += [(n, i) for i in range(n.shape[0])]
    tail = notes[0].shape[1] - height
    stacked = [n[i, height:, :] for n, i in rows_of]
    stacked.append(jnp.zeros((-(-shards * tail // lanes) * lanes - shards * tail, lanes), f32))
    turned[...] = jnp.transpose(jnp.concatenate(stacked, axis=0))
    first = me * span
    block = turned[pl.ds(pl.multiple_of(lax.rem(first, lanes), span), span), :]
    lane = lax.broadcasted_iota(jnp.int32, block.shape, 1)
    pick = lax.div(first, lanes)

    def column(at):
        return jnp.sum(jnp.where(lane == at + pick, block, 0.0), axis=1, keepdims=True)

    means = [column(k * tail) for k in range(shards)]
    spreads = [column(k * tail + many) for k in range(shards)]
    mean = tree(means, jnp.add) / shards
    spread = tree(spreads, jnp.add) / width
    spread += tree([(m - mean) * (m - mean) for m in means], jnp.add) / shards
    inverse = lax.rsqrt(spread + norm_epsilon)
    pieces = []
    squares = jnp.zeros((span, lanes), f32)
    for j in range(height):
        at = slice(j * lanes, (j + 1) * lanes)
        value = own[:, at]
        for part in parts:
            value += part[:, at].astype(f32)
        for k, (n, i) in enumerate(rows_of):
            value += (means[k] - mean) * n[i, j : j + 1, :]
        value *= inverse
        squares += value * value
        pieces.append(value)
    scale = lax.rsqrt(jnp.sum(squares, axis=1, keepdims=True) + unit_epsilon)
    for j in range(height):
        unit_out[:, j * lanes : (j + 1) * lanes] = (pieces[j] * scale).astype(bf16)


def scores_kernel(halves, shards, multiplier, left, right, *rest):
    owns = rest[:4]
    others = rest[4:-4]
    scores_out, column_out, gathered, mine = rest[-4:]
    span = owns[0].shape[0]
    fars = shards // 2
    dp, mp = lax.axis_index("dp"), lax.axis_index("mp")
    core, near = lax.rem(dp, 2), lax.rem(mp, 2)
    half, far = lax.div(dp, 2), lax.div(mp, 2)
    for h in range(halves):
        for m in range(fars):
            at = ((half ^ h) * fars + (far ^ m)) * span
            gathered[pl.ds(pl.multiple_of(at, span), span), :] = others[h * fars + m][...]
    for c in range(2):
        for n in range(2):
            at = ((core ^ c) * 2 + (near ^ n)) * span
            mine[pl.ds(pl.multiple_of(at, span), span), :] = owns[c * 2 + n][...]
    scores = multiplier[0] * lax.dot_general(
        mine[...], gathered[...], (((1,), (1,)), ((), ())), preferred_element_type=f32
    )
    scores_out[...] = scores
    column_peak = jnp.max(scores, axis=0, keepdims=True)
    column_part = column_peak + jnp.log(
        jnp.sum(jnp.exp(scores - column_peak), axis=0, keepdims=True)
    )
    matched = left[...] == right[...]
    target = jnp.sum(jnp.where(matched, scores, 0.0), axis=0, keepdims=True)
    row = lax.broadcasted_iota(jnp.int32, column_out.shape, 0)
    column_out[...] = jnp.where(row == 0, column_part, jnp.where(row == 1, target, 0.0))


def rows_kernel(scores, out):
    values = scores[...]
    peak = jnp.max(values, axis=1, keepdims=True)
    part = peak + jnp.log(jnp.sum(jnp.exp(values - peak), axis=1, keepdims=True))
    out[...] = jnp.transpose(jnp.broadcast_to(part, (values.shape[0], lanes)))[0:1, :]


def merge_rows_kernel(row, row_other, out):
    out[...] = jnp.broadcast_to(log_add(row[...], row_other[...]), out.shape)


def merge_columns_kernel(column, column_other, after, out):
    out[...] = merge_columns(column[0:2, :], column_other[0:2, :])


def grads_kernel(
    multiplier, left, right, scores, gathered, column, column_other, *rest
):
    row, row_other, sent_out, loss_out, weights = rest
    rows, width_out = sent_out.shape[0], gathered.shape[1]
    core = lax.rem(lax.axis_index("dp"), 2)
    row_total = log_add(row[0:1, :], row_other[0:1, :])
    column_both = merge_columns(column[...], column_other[...])
    column_total = column_both[0:1, :]
    loss = jnp.sum(column_total - column_both[1:2, :], axis=1, keepdims=True)
    loss = jnp.broadcast_to(loss, loss_out.shape)
    loss_out[...] = loss
    sent_out[:, width_out:] = split_rows(loss, rows)
    row_total = jnp.transpose(jnp.broadcast_to(row_total, (lanes, row_total.shape[1])))[:, 0:1]
    matched = left[...] == right[...]
    values = scores[...]
    weights[...] = (
        multiplier[0]
        * (
            jnp.exp(values - row_total)
            + jnp.exp(values - column_total)
            - jnp.where(matched, 2.0, 0.0)
        )
    ).astype(bf16)
    part = weights[pl.ds(pl.multiple_of((1 - core) * rows, rows), rows), :]
    sent_out[:, :width_out] = jnp.dot(
        part, gathered[...], preferred_element_type=f32
    ).astype(bf16)


def kept_kernel(weights, gathered, out):
    rows = out.shape[0]
    core = lax.rem(lax.axis_index("dp"), 2)
    part = weights[pl.ds(pl.multiple_of(core * rows, rows), rows), :]
    out[...] = jnp.dot(part, gathered[...], preferred_element_type=f32)


def halve_kernel(kept, received, loss, own_out, sent_out, loss_out):
    rows, width_out = own_out.shape
    near = lax.rem(lax.axis_index("mp"), 2)
    mine = pl.ds(pl.multiple_of(near * rows, rows), rows)
    yours = pl.ds(pl.multiple_of((1 - near) * rows, rows), rows)
    loss = loss[...] + jnp.sum(received[:, width_out:].astype(f32), axis=0, keepdims=True)
    loss_out[...] = loss
    own_out[...] = kept[mine, :] + received[mine, :width_out].astype(f32)
    sent_out[:, :width_out] = (kept[yours, :] + received[yours, :width_out].astype(f32)).astype(bf16)
    sent_out[:, width_out:] = split_rows(loss, rows)


def total_kernel(scale, own, received, loss, there, there_near, out, loss_out):
    width_out = own.shape[1]
    out[...] = own[...] + received[:, :width_out].astype(f32)
    near = jnp.sum(received[:, width_out:].astype(f32), axis=0, keepdims=True)
    loss = (loss[...] + near) + (there[...] + there_near[...])
    loss_out[...] = loss[:, 0:1] * scale


def body(
    image_features, text_features, image_gain, text_gain, image_proj, text_proj, pair, logit_scale
):
    rows = image_features.shape[0]
    shards = lax.axis_size("mp")
    owners = lax.axis_size("dp")
    halves, fars = owners // 2, shards // 2
    span = rows // shards
    width_out = image_proj.shape[1]
    group = lax.axis_index("group")
    me = lax.axis_index("mp")
    owner = lax.axis_index("dp")
    many = rows // lanes
    note_height = -(-(width_out // lanes + 2 * many) // 8) * 8
    shape = jax.ShapeDtypeStruct

    def project(x, gain, p):
        width = x.shape[1]
        return pl.pallas_call(
            functools.partial(project_kernel, shards),
            out_shape=[
                shape((span, width_out), f32),
                shape(((fars - 1) * span, width_out), f32),
                shape((span, width_out), bf16),
                shape(((fars - 1) * span, width_out), bf16),
                shape((1, note_height, lanes), f32),
            ],
            in_specs=[HBM, VMEM, HBM],
            out_specs=[VMEM] * 5,
            scratch_shapes=[
                pltpu.VMEM((rows, width), bf16),
                pltpu.VMEM((width, width_out), bf16),
                pltpu.VMEM((rows + 16, width), bf16),
                pltpu.VMEM((rows + 16, width_out), f32),
                pltpu.SemaphoreType.DMA((X_CUTS + max(1, width // P_STEP),)),
            ],
            compiler_params=PARAMS_P,
            name="project",
        )(x, gain, p)

    own, kept, near_part, far_part, note = lax.cond(
        group == 0,
        lambda: project(text_features, text_gain, text_proj),
        lambda: project(image_features, image_gain, image_proj),
    )
    far_other = exchange(far_part, "mp", 1)
    note_other = exchange(note, "mp", 1)
    *pairs, near_part = pl.pallas_call(
        pair_kernel,
        out_shape=[shape((span, width_out), bf16)] * fars,
        in_specs=[VMEM] * 3,
        out_specs=[VMEM] * fars,
        compiler_params=PARAMS,
        name="pair",
    )(kept, far_other, near_part)
    both = pl.pallas_call(
        both_kernel,
        out_shape=shape((2, note_height, lanes), f32),
        in_specs=[VMEM] * 2,
        out_specs=VMEM,
        compiler_params=PARAMS,
        name="both",
    )(note, note_other)
    parts = []
    notes = [both]
    for m in range(1, fars):
        parts.append(exchange(pairs[m - 1], "mp", 2 * m))
        notes.append(exchange(both, "mp", 2 * m))
    parts.append(exchange(near_part, "mp", 1))

    core, near = owner % 2, me % 2
    half, far = owner // 2, me // 2
    numbers = jnp.arange(owners * rows, dtype=jnp.int32)
    cut = (halves, 2, fars, 2, span)

    def of_rows(v):
        return lax.dynamic_slice(
            v.reshape(cut), (half, 0, far, 0, 0), (1, 2, 1, 2, span)
        ).reshape(4 * span, 1)

    def of_columns(v):
        return lax.dynamic_slice(
            v.reshape(cut), (0, core, 0, near, 0), (halves, 1, fars, 1, span)
        ).reshape(1, halves * fars * span)

    image_rows = group == 0
    left = of_rows(jnp.where(image_rows, pair, numbers))
    right = of_columns(jnp.where(image_rows, numbers, pair))
    row_count, column_count = 4 * span, halves * fars * span
    multiplier = logit_scale.reshape(1)

    unit = pl.pallas_call(
        functools.partial(
            finish_kernel,
            shards,
            many,
            (text_features.shape[1] * shards, image_features.shape[1] * shards),
        ),
        out_shape=shape((span, width_out), bf16),
        in_specs=[VMEM] * (1 + len(parts) + len(notes) + 2),
        out_specs=VMEM,
        scratch_shapes=[
            pltpu.VMEM(
                (
                    lanes,
                    -(-shards * (note_height - width_out // lanes) // lanes) * lanes,
                ),
                f32,
            )
        ],
        compiler_params=PARAMS,
        name="finish",
    )(own, *parts, *notes, left, right)

    others = [unit] + [exchange(unit, "mp", m * 2) for m in range(1, fars)]
    owns = [cross_exchange(unit, 0), cross_exchange(unit, 1)]
    blocks = list(others)
    for h in range(1, halves):
        blocks += [exchange(b, "dp", h * 2) for b in others]
    owns += [exchange(b, "dp", 1) for b in owns]

    scores, column_part, gathered = pl.pallas_call(
        functools.partial(scores_kernel, halves, shards),
        out_shape=[
            shape((row_count, column_count), f32),
            shape((COLUMN_COPIES, column_count), f32),
            shape((column_count, width_out), bf16),
        ],
        in_specs=[SMEM] + [VMEM] * (2 + 4 + halves * fars),
        out_specs=[VMEM] * 3,
        scratch_shapes=[pltpu.VMEM((row_count, width_out), bf16)],
        compiler_params=PARAMS,
        name="scores",
    )(multiplier, left, right, *owns, *blocks)

    def merged(kernel, height, *operands):
        return pl.pallas_call(
            kernel,
            out_shape=shape((height, operands[0].shape[1]), f32),
            in_specs=[VMEM] * len(operands),
            out_specs=VMEM,
            compiler_params=PARAMS,
            name="merge",
        )(*operands)

    row_part = pl.pallas_call(
        rows_kernel,
        out_shape=shape((1, row_count), f32),
        in_specs=[VMEM],
        out_specs=VMEM,
        compiler_params=PARAMS,
        name="rows",
    )(scores)

    column_steps = [("dp", 2 << i) for i in range((halves - 1).bit_length())]
    column_steps += [("mp", 2 << i) for i in range((fars - 1).bit_length())]
    row, column = row_part, column_part
    row = merged(merge_rows_kernel, ROW_COPIES, row, exchange(row, "dp", 1))
    row_other = exchange(row, "mp", 1)
    for axis, distance in column_steps[:-1]:
        column = merged(merge_columns_kernel, 2, column, exchange(column, axis, distance), row)
    column_other = exchange(column, *column_steps[-1])

    sent, loss, weights = pl.pallas_call(
        grads_kernel,
        out_shape=[
            shape((2 * span, width_out + lanes), bf16),
            shape((1, lanes), f32),
            shape((row_count, column_count), bf16),
        ],
        in_specs=[SMEM] + [VMEM] * 8,
        out_specs=[VMEM] * 3,
        compiler_params=PARAMS,
        name="grads",
    )(multiplier, left, right, scores, gathered, column, column_other, row, row_other)
    kept = pl.pallas_call(
        kept_kernel,
        out_shape=shape((2 * span, width_out), f32),
        in_specs=[VMEM] * 2,
        out_specs=VMEM,
        compiler_params=PARAMS,
        name="kept",
    )(weights, gathered)
    own, sent, loss = pl.pallas_call(
        halve_kernel,
        out_shape=[
            shape((span, width_out), f32),
            shape((span, width_out + lanes), bf16),
            shape((1, lanes), f32),
        ],
        in_specs=[VMEM] * 3,
        out_specs=[VMEM] * 3,
        compiler_params=PARAMS,
        name="halve",
    )(kept, exchange(sent, "dp", 1), loss)
    there, there_near = cross_exchange(loss, 0), cross_exchange(loss, 1)
    grads, loss = pl.pallas_call(
        functools.partial(total_kernel, 1.0 / (2.0 * owners * rows)),
        out_shape=[shape((span, width_out), f32), shape((1, 1), f32)],
        in_specs=[VMEM] * 5,
        out_specs=[VMEM] * 2,
        compiler_params=PARAMS,
        name="total",
    )(own, exchange(sent, "mp", 1), loss, there, there_near)
    return (grads[None, :, :], loss[0, 0])


def solution(mesh):
    in_specs = (
        P("dp", "mp"),
        P("dp", "mp"),
        P("mp"),
        P("mp"),
        P("mp", None),
        P("mp", None),
        P(),
        P(),
    )
    out_specs = (P("group", ("dp", "mp"), None), P())
    return jax.shard_map(body, mesh=mesh, in_specs=in_specs, out_specs=out_specs, check_vma=False)
```

```python
import functools

import jax
import jax.numpy as jnp
from jax import lax
from jax.experimental import pallas as pl
from jax.experimental.pallas import tpu as pltpu
from jax.sharding import PartitionSpec as P

norm_epsilon = 1e-05
unit_epsilon = 1e-06
lanes = 128
X_CUTS = 1
R_BLOCK = 16
ROW_COPIES = 8
COLUMN_COPIES = 8
P_STEP = 512
VMEM = pl.BlockSpec(memory_space=pltpu.VMEM)
SMEM = pl.BlockSpec(memory_space=pltpu.SMEM)
HBM = pl.BlockSpec(memory_space=pltpu.HBM)
PARAMS_P = pltpu.CompilerParams(vmem_limit_bytes=55500000)
PARAMS = pltpu.CompilerParams(vmem_limit_bytes=48 * 1024 * 1024)
f32 = jnp.float32
bf16 = jnp.bfloat16


def exchange(shard, axis, distance):
    return lax.ppermute(shard, axis, [(i, i ^ distance) for i in range(lax.axis_size(axis))])


def cross_exchange(shard, distance):
    count = lax.axis_size("mp")
    pairs = [
        (side * count + i, (1 - side) * count + (i ^ distance))
        for side in range(2)
        for i in range(count)
    ]
    return lax.ppermute(shard, ("group", "mp"), pairs)


def tree(values, combine):
    values = list(values)
    while len(values) > 1:
        values = [combine(values[i], values[i + 1]) for i in range(0, len(values), 2)]
    return values[0]


def log_add(a, b):
    peak = jnp.maximum(a, b)
    return peak + jnp.log1p(jnp.exp(jnp.minimum(a, b) - peak))


def merge_columns(a, b):
    row = lax.broadcasted_iota(jnp.int32, a.shape, 0)
    return jnp.where(row == 0, log_add(a, b), a + b)


def split_rows(value, rows):
    high = value.astype(bf16).astype(f32)
    middle = (value - high).astype(bf16).astype(f32)
    low = value - high - middle
    row = lax.broadcasted_iota(jnp.int32, (rows, value.shape[1]), 0)
    parts = jnp.where(row == 0, high, jnp.where(row == 1, middle, jnp.where(row == 2, low, 0.0)))
    return parts.astype(bf16)


def project_kernel(shards, x_hbm, gain, p_hbm, *rest):
    own_out, kept_out, near_out, far_out, note, x_buf, p_buf, scaled, total, sems = rest
    rows, width = x_buf.shape
    span = rows // shards
    width_out = total.shape[1]
    me = lax.axis_index("mp")
    some = rows // X_CUTS
    x_copies = []
    for c in range(X_CUTS):
        at = pl.ds(c * some, some)
        copy = pltpu.make_async_copy(x_hbm.at[at], x_buf.at[at], sems.at[c])
        copy.start()
        x_copies.append(copy)
    cuts = max(1, width // P_STEP)
    deep = width // cuts
    copies = []
    for c in range(cuts):
        at = pl.ds(c * deep, deep)
        copy = pltpu.make_async_copy(p_hbm.at[at], p_buf.at[at], sems.at[X_CUTS + c])
        copy.start()
        copies.append(copy)
    g = gain[...].reshape(1, width)
    scaled[rows:, :] = split_rows(g, 16)
    packs = []
    lane = lax.broadcasted_iota(jnp.int32, (R_BLOCK, lanes), 1)
    for c in range(X_CUTS):
        x_copies[c].wait()
        for r in range(c * some, (c + 1) * some, R_BLOCK):
            at = slice(r, r + R_BLOCK)
            values = x_buf[at, :].astype(f32)
            mean = jnp.sum(values, axis=1, keepdims=True) / width
            centred = values - mean
            spread = jnp.sum(centred * centred, axis=1, keepdims=True)
            scaled[at, :] = (centred * g).astype(bf16)
            packs.append(jnp.where(lane == 0, mean, jnp.where(lane == 1, spread, 0.0)))
    stats = jnp.transpose(jnp.concatenate(packs, axis=0))
    height = width_out // lanes
    many = rows // lanes
    for j in range(many):
        for kind in range(2):
            at = height + kind * many + j
            note[0, at : at + 1, :] = stats[kind : kind + 1, j * lanes : (j + 1) * lanes]
    for c in range(cuts):
        copies[c].wait()
        at = slice(c * deep, (c + 1) * deep)
        product = jnp.dot(scaled[:, at], p_buf[at, :], preferred_element_type=f32)
        if c == 0:
            total[...] = product
        else:
            total[...] += product
    offset = jnp.sum(total[rows:, :], axis=0, keepdims=True)
    for j in range(height):
        note[0, j : j + 1, :] = offset[:, j * lanes : (j + 1) * lanes]

    def block(distance):
        return total[pl.ds(pl.multiple_of((me ^ distance) * span, span), span), :]

    for m in range(1, shards // 2):
        at = slice((m - 1) * span, m * span)
        far_out[at, :] = block(2 * m + 1).astype(bf16)
        kept_out[at, :] = block(2 * m)
    near_out[...] = block(1).astype(bf16)
    own_out[...] = block(0)


def pair_kernel(kept, received, near, *rest):
    *outs, near_out = rest
    near_out[...] = near[...]
    span = outs[0].shape[0]
    for m, out in enumerate(outs):
        at = slice(m * span, (m + 1) * span)
        out[...] = (kept[at, :] + received[at, :].astype(f32)).astype(bf16)


def both_kernel(note, note_other, notes):
    notes[0] = note[0]
    notes[1] = note_other[0]


def finish_kernel(shards, many, widths, own, *rest):
    fars = shards // 2
    parts = rest[:fars]
    notes = rest[fars:-4]
    unit_out, turned = rest[-2:]
    span, width_out = own.shape
    height = width_out // lanes
    me = lax.axis_index("mp")
    width = jnp.where(lax.axis_index("group") == 0, widths[0], widths[1]).astype(f32)
    rows_of = []
    for n in notes:
        rows_of += [(n, i) for i in range(n.shape[0])]
    tail = notes[0].shape[1] - height
    stacked = [n[i, height:, :] for n, i in rows_of]
    stacked.append(jnp.zeros((-(-shards * tail // lanes) * lanes - shards * tail, lanes), f32))
    turned[...] = jnp.transpose(jnp.concatenate(stacked, axis=0))
    first = me * span
    block = turned[pl.ds(pl.multiple_of(lax.rem(first, lanes), span), span), :]
    lane = lax.broadcasted_iota(jnp.int32, block.shape, 1)
    pick = lax.div(first, lanes)

    def column(at):
        return jnp.sum(jnp.where(lane == at + pick, block, 0.0), axis=1, keepdims=True)

    means = [column(k * tail) for k in range(shards)]
    spreads = [column(k * tail + many) for k in range(shards)]
    mean = tree(means, jnp.add) / shards
    spread = tree(spreads, jnp.add) / width
    spread += tree([(m - mean) * (m - mean) for m in means], jnp.add) / shards
    inverse = lax.rsqrt(spread + norm_epsilon)
    pieces = []
    squares = jnp.zeros((span, lanes), f32)
    for j in range(height):
        at = slice(j * lanes, (j + 1) * lanes)
        value = own[:, at]
        for part in parts:
            value += part[:, at].astype(f32)
        for k, (n, i) in enumerate(rows_of):
            value += (means[k] - mean) * n[i, j : j + 1, :]
        value *= inverse
        squares += value * value
        pieces.append(value)
    scale = lax.rsqrt(jnp.sum(squares, axis=1, keepdims=True) + unit_epsilon)
    for j in range(height):
        unit_out[:, j * lanes : (j + 1) * lanes] = (pieces[j] * scale).astype(bf16)


def scores_kernel(halves, shards, multiplier, left, right, *rest):
    owns = rest[:4]
    others = rest[4:-4]
    scores_out, column_out, gathered, mine = rest[-4:]
    span = owns[0].shape[0]
    fars = shards // 2
    dp, mp = lax.axis_index("dp"), lax.axis_index("mp")
    core, near = lax.rem(dp, 2), lax.rem(mp, 2)
    half, far = lax.div(dp, 2), lax.div(mp, 2)
    for h in range(halves):
        for m in range(fars):
            at = ((half ^ h) * fars + (far ^ m)) * span
            gathered[pl.ds(pl.multiple_of(at, span), span), :] = others[h * fars + m][...]
    for c in range(2):
        for n in range(2):
            at = ((core ^ c) * 2 + (near ^ n)) * span
            mine[pl.ds(pl.multiple_of(at, span), span), :] = owns[c * 2 + n][...]
    scores = multiplier[0] * lax.dot_general(
        mine[...], gathered[...], (((1,), (1,)), ((), ())), preferred_element_type=f32
    )
    scores_out[...] = scores
    column_peak = jnp.max(scores, axis=0, keepdims=True)
    column_part = column_peak + jnp.log(
        jnp.sum(jnp.exp(scores - column_peak), axis=0, keepdims=True)
    )
    matched = left[...] == right[...]
    target = jnp.sum(jnp.where(matched, scores, 0.0), axis=0, keepdims=True)
    row = lax.broadcasted_iota(jnp.int32, column_out.shape, 0)
    column_out[...] = jnp.where(row == 0, column_part, jnp.where(row == 1, target, 0.0))


def rows_kernel(scores, out):
    values = scores[...]
    peak = jnp.max(values, axis=1, keepdims=True)
    part = peak + jnp.log(jnp.sum(jnp.exp(values - peak), axis=1, keepdims=True))
    out[...] = jnp.transpose(jnp.broadcast_to(part, (values.shape[0], lanes)))[0:1, :]


def merge_rows_kernel(row, row_other, out):
    out[...] = jnp.broadcast_to(log_add(row[...], row_other[...]), out.shape)


def merge_columns_kernel(column, column_other, after, out):
    out[...] = merge_columns(column[0:2, :], column_other[0:2, :])


def grads_kernel(
    multiplier, left, right, scores, gathered, column, column_other, *rest
):
    row, row_other, sent_out, loss_out, weights = rest
    rows, width_out = sent_out.shape[0], gathered.shape[1]
    core = lax.rem(lax.axis_index("dp"), 2)
    row_total = log_add(row[0:1, :], row_other[0:1, :])
    column_both = merge_columns(column[...], column_other[...])
    column_total = column_both[0:1, :]
    loss = jnp.sum(column_total - column_both[1:2, :], axis=1, keepdims=True)
    loss = jnp.broadcast_to(loss, loss_out.shape)
    loss_out[...] = loss
    sent_out[:, width_out:] = split_rows(loss, rows)
    row_total = jnp.transpose(jnp.broadcast_to(row_total, (lanes, row_total.shape[1])))[:, 0:1]
    matched = left[...] == right[...]
    values = scores[...]
    weights[...] = (
        multiplier[0]
        * (
            jnp.exp(values - row_total)
            + jnp.exp(values - column_total)
            - jnp.where(matched, 2.0, 0.0)
        )
    ).astype(bf16)
    part = weights[pl.ds(pl.multiple_of((1 - core) * rows, rows), rows), :]
    sent_out[:, :width_out] = jnp.dot(
        part, gathered[...], preferred_element_type=f32
    ).astype(bf16)


def kept_kernel(weights, gathered, out):
    rows = out.shape[0]
    core = lax.rem(lax.axis_index("dp"), 2)
    part = weights[pl.ds(pl.multiple_of(core * rows, rows), rows), :]
    out[...] = jnp.dot(part, gathered[...], preferred_element_type=f32)


def halve_kernel(kept, received, loss, own_out, sent_out, loss_out):
    rows, width_out = own_out.shape
    near = lax.rem(lax.axis_index("mp"), 2)
    mine = pl.ds(pl.multiple_of(near * rows, rows), rows)
    yours = pl.ds(pl.multiple_of((1 - near) * rows, rows), rows)
    loss = loss[...] + jnp.sum(received[:, width_out:].astype(f32), axis=0, keepdims=True)
    loss_out[...] = loss
    own_out[...] = kept[mine, :] + received[mine, :width_out].astype(f32)
    sent_out[:, :width_out] = (kept[yours, :] + received[yours, :width_out].astype(f32)).astype(bf16)
    sent_out[:, width_out:] = split_rows(loss, rows)


def body(
    image_features, text_features, image_gain, text_gain, image_proj, text_proj, pair, logit_scale
):
    rows = image_features.shape[0]
    shards = lax.axis_size("mp")
    owners = lax.axis_size("dp")
    halves, fars = owners // 2, shards // 2
    span = rows // shards
    width_out = image_proj.shape[1]
    group = lax.axis_index("group")
    me = lax.axis_index("mp")
    owner = lax.axis_index("dp")
    many = rows // lanes
    note_height = -(-(width_out // lanes + 2 * many) // 8) * 8
    shape = jax.ShapeDtypeStruct

    def project(x, gain, p):
        width = x.shape[1]
        return pl.pallas_call(
            functools.partial(project_kernel, shards),
            out_shape=[
                shape((span, width_out), f32),
                shape(((fars - 1) * span, width_out), f32),
                shape((span, width_out), bf16),
                shape(((fars - 1) * span, width_out), bf16),
                shape((1, note_height, lanes), f32),
            ],
            in_specs=[HBM, VMEM, HBM],
            out_specs=[VMEM] * 5,
            scratch_shapes=[
                pltpu.VMEM((rows, width), bf16),
                pltpu.VMEM((width, width_out), bf16),
                pltpu.VMEM((rows + 16, width), bf16),
                pltpu.VMEM((rows + 16, width_out), f32),
                pltpu.SemaphoreType.DMA((X_CUTS + max(1, width // P_STEP),)),
            ],
            compiler_params=PARAMS_P,
            name="project",
        )(x, gain, p)

    own, kept, near_part, far_part, note = lax.cond(
        group == 0,
        lambda: project(text_features, text_gain, text_proj),
        lambda: project(image_features, image_gain, image_proj),
    )
    far_other = exchange(far_part, "mp", 1)
    note_other = exchange(note, "mp", 1)
    *pairs, near_part = pl.pallas_call(
        pair_kernel,
        out_shape=[shape((span, width_out), bf16)] * fars,
        in_specs=[VMEM] * 3,
        out_specs=[VMEM] * fars,
        compiler_params=PARAMS,
        name="pair",
    )(kept, far_other, near_part)
    both = pl.pallas_call(
        both_kernel,
        out_shape=shape((2, note_height, lanes), f32),
        in_specs=[VMEM] * 2,
        out_specs=VMEM,
        compiler_params=PARAMS,
        name="both",
    )(note, note_other)
    parts = []
    notes = [both]
    for m in range(1, fars):
        parts.append(exchange(pairs[m - 1], "mp", 2 * m))
        notes.append(exchange(both, "mp", 2 * m))
    parts.append(exchange(near_part, "mp", 1))

    core, near = owner % 2, me % 2
    half, far = owner // 2, me // 2
    numbers = jnp.arange(owners * rows, dtype=jnp.int32)
    cut = (halves, 2, fars, 2, span)

    def of_rows(v):
        return lax.dynamic_slice(
            v.reshape(cut), (half, 0, far, 0, 0), (1, 2, 1, 2, span)
        ).reshape(4 * span, 1)

    def of_columns(v):
        return lax.dynamic_slice(
            v.reshape(cut), (0, core, 0, near, 0), (halves, 1, fars, 1, span)
        ).reshape(1, halves * fars * span)

    image_rows = group == 0
    left = of_rows(jnp.where(image_rows, pair, numbers))
    right = of_columns(jnp.where(image_rows, numbers, pair))
    row_count, column_count = 4 * span, halves * fars * span
    multiplier = logit_scale.reshape(1)

    unit = pl.pallas_call(
        functools.partial(
            finish_kernel,
            shards,
            many,
            (text_features.shape[1] * shards, image_features.shape[1] * shards),
        ),
        out_shape=shape((span, width_out), bf16),
        in_specs=[VMEM] * (1 + len(parts) + len(notes) + 2),
        out_specs=VMEM,
        scratch_shapes=[
            pltpu.VMEM(
                (
                    lanes,
                    -(-shards * (note_height - width_out // lanes) // lanes) * lanes,
                ),
                f32,
            )
        ],
        compiler_params=PARAMS,
        name="finish",
    )(own, *parts, *notes, left, right)

    others = [unit] + [exchange(unit, "mp", m * 2) for m in range(1, fars)]
    owns = [cross_exchange(unit, 0), cross_exchange(unit, 1)]
    blocks = list(others)
    for h in range(1, halves):
        blocks += [exchange(b, "dp", h * 2) for b in others]
    owns += [exchange(b, "dp", 1) for b in owns]

    scores, column_part, gathered = pl.pallas_call(
        functools.partial(scores_kernel, halves, shards),
        out_shape=[
            shape((row_count, column_count), f32),
            shape((COLUMN_COPIES, column_count), f32),
            shape((column_count, width_out), bf16),
        ],
        in_specs=[SMEM] + [VMEM] * (2 + 4 + halves * fars),
        out_specs=[VMEM] * 3,
        scratch_shapes=[pltpu.VMEM((row_count, width_out), bf16)],
        compiler_params=PARAMS,
        name="scores",
    )(multiplier, left, right, *owns, *blocks)

    def merged(kernel, height, *operands):
        return pl.pallas_call(
            kernel,
            out_shape=shape((height, operands[0].shape[1]), f32),
            in_specs=[VMEM] * len(operands),
            out_specs=VMEM,
            compiler_params=PARAMS,
            name="merge",
        )(*operands)

    row_part = pl.pallas_call(
        rows_kernel,
        out_shape=shape((1, row_count), f32),
        in_specs=[VMEM],
        out_specs=VMEM,
        compiler_params=PARAMS,
        name="rows",
    )(scores)

    column_steps = [("dp", 2 << i) for i in range((halves - 1).bit_length())]
    column_steps += [("mp", 2 << i) for i in range((fars - 1).bit_length())]
    row, column = row_part, column_part
    row = merged(merge_rows_kernel, ROW_COPIES, row, exchange(row, "dp", 1))
    row_other = exchange(row, "mp", 1)
    for axis, distance in column_steps[:-1]:
        column = merged(merge_columns_kernel, 2, column, exchange(column, axis, distance), row)
    column_other = exchange(column, *column_steps[-1])

    sent, loss, weights = pl.pallas_call(
        grads_kernel,
        out_shape=[
            shape((2 * span, width_out + lanes), bf16),
            shape((1, lanes), f32),
            shape((row_count, column_count), bf16),
        ],
        in_specs=[SMEM] + [VMEM] * 8,
        out_specs=[VMEM] * 3,
        compiler_params=PARAMS,
        name="grads",
    )(multiplier, left, right, scores, gathered, column, column_other, row, row_other)
    kept = pl.pallas_call(
        kept_kernel,
        out_shape=shape((2 * span, width_out), f32),
        in_specs=[VMEM] * 2,
        out_specs=VMEM,
        compiler_params=PARAMS,
        name="kept",
    )(weights, gathered)
    own, sent, loss = pl.pallas_call(
        halve_kernel,
        out_shape=[
            shape((span, width_out), f32),
            shape((span, width_out + lanes), bf16),
            shape((1, lanes), f32),
        ],
        in_specs=[VMEM] * 3,
        out_specs=[VMEM] * 3,
        compiler_params=PARAMS,
        name="halve",
    )(kept, exchange(sent, "dp", 1), loss)
    there, there_near = cross_exchange(loss, 0), cross_exchange(loss, 1)
    received = exchange(sent, "mp", 1)
    grads = own + received[:, :width_out].astype(f32)
    near_loss = jnp.sum(received[:, width_out:].astype(f32), axis=0, keepdims=True)
    loss = ((loss + near_loss) + (there + there_near)) * (1.0 / (2.0 * owners * rows))
    return (grads[None, :, :], loss[0, 0])


def solution(mesh):
    in_specs = (
        P("dp", "mp"),
        P("dp", "mp"),
        P("mp"),
        P("mp"),
        P("mp", None),
        P("mp", None),
        P(),
        P(),
    )
    out_specs = (P("group", ("dp", "mp"), None), P())
    return jax.shard_map(body, mesh=mesh, in_specs=in_specs, out_specs=out_specs, check_vma=False)
```

```python
import functools

import jax
import jax.numpy as jnp
from jax import lax
from jax.experimental import pallas as pl
from jax.experimental.pallas import tpu as pltpu
from jax.sharding import PartitionSpec as P

norm_epsilon = 1e-05
unit_epsilon = 1e-06
lanes = 128
X_CUTS = 1
R_BLOCK = 16
ROW_COPIES = 8
COLUMN_COPIES = 8
P_STEP = 512
VMEM = pl.BlockSpec(memory_space=pltpu.VMEM)
SMEM = pl.BlockSpec(memory_space=pltpu.SMEM)
HBM = pl.BlockSpec(memory_space=pltpu.HBM)
PARAMS_P = pltpu.CompilerParams(vmem_limit_bytes=55500000)
PARAMS = pltpu.CompilerParams(vmem_limit_bytes=48 * 1024 * 1024)
f32 = jnp.float32
bf16 = jnp.bfloat16


def exchange(shard, axis, distance):
    return lax.ppermute(shard, axis, [(i, i ^ distance) for i in range(lax.axis_size(axis))])


def cross_exchange(shard, distance):
    count = lax.axis_size("mp")
    pairs = [
        (side * count + i, (1 - side) * count + (i ^ distance))
        for side in range(2)
        for i in range(count)
    ]
    return lax.ppermute(shard, ("group", "mp"), pairs)


def tree(values, combine):
    values = list(values)
    while len(values) > 1:
        values = [combine(values[i], values[i + 1]) for i in range(0, len(values), 2)]
    return values[0]


def log_add(a, b):
    peak = jnp.maximum(a, b)
    return peak + jnp.log1p(jnp.exp(jnp.minimum(a, b) - peak))


def merge_columns(a, b):
    row = lax.broadcasted_iota(jnp.int32, a.shape, 0)
    return jnp.where(row == 0, log_add(a, b), a + b)


def split_rows(value, rows):
    high = value.astype(bf16).astype(f32)
    middle = (value - high).astype(bf16).astype(f32)
    low = value - high - middle
    row = lax.broadcasted_iota(jnp.int32, (rows, value.shape[1]), 0)
    parts = jnp.where(row == 0, high, jnp.where(row == 1, middle, jnp.where(row == 2, low, 0.0)))
    return parts.astype(bf16)


def project_kernel(shards, x_hbm, gain, p_hbm, *rest):
    own_out, kept_out, near_out, far_out, note, x_buf, p_buf, scaled, total, stat, sems = rest
    rows, width = x_buf.shape
    span = rows // shards
    width_out = total.shape[1]
    me = lax.axis_index("mp")
    some = rows // X_CUTS
    x_copies = []
    for c in range(X_CUTS):
        at = pl.ds(c * some, some)
        copy = pltpu.make_async_copy(x_hbm.at[at], x_buf.at[at], sems.at[c])
        copy.start()
        x_copies.append(copy)
    cuts = max(1, width // P_STEP)
    deep = width // cuts
    copies = []
    for c in range(cuts):
        at = pl.ds(c * deep, deep)
        copy = pltpu.make_async_copy(p_hbm.at[at], p_buf.at[at], sems.at[X_CUTS + c])
        copy.start()
        copies.append(copy)
    g = gain[...].reshape(1, width)
    scaled[rows:, :] = split_rows(g, 16)
    lane = lax.broadcasted_iota(jnp.int32, (R_BLOCK, lanes), 1)
    for copy in x_copies:
        copy.wait()
    for k in range(shards):
        for r in range(0, span, R_BLOCK):
            at = pl.ds(pl.multiple_of((me ^ k) * span + r, R_BLOCK), R_BLOCK)
            values = x_buf[at, :].astype(f32)
            mean = jnp.sum(values, axis=1, keepdims=True) / width
            centred = values - mean
            spread = jnp.sum(centred * centred, axis=1, keepdims=True)
            scaled[k * span + r : k * span + r + R_BLOCK, :] = (centred * g).astype(bf16)
            stat[at, :] = jnp.where(lane == 0, mean, jnp.where(lane == 1, spread, 0.0))
    stats = jnp.transpose(stat[...])
    height = width_out // lanes
    many = rows // lanes
    for j in range(many):
        for kind in range(2):
            at = height + kind * many + j
            note[0, at : at + 1, :] = stats[kind : kind + 1, j * lanes : (j + 1) * lanes]
    for c in range(cuts):
        copies[c].wait()
        at = slice(c * deep, (c + 1) * deep)
        product = jnp.dot(scaled[:, at], p_buf[at, :], preferred_element_type=f32)
        if c < cuts - 1:
            total[...] = product if c == 0 else total[...] + product

    def block(first, size):
        at = slice(first, first + size)
        return product[at] if cuts == 1 else total[at, :] + product[at]

    for m in range(1, shards // 2):
        at = slice((m - 1) * span, m * span)
        far_out[at, :] = block((2 * m + 1) * span, span).astype(bf16)
        kept_out[at, :] = block(2 * m * span, span)
    near_out[...] = block(span, span).astype(bf16)
    own_out[...] = block(0, span)
    offset = jnp.sum(block(rows, 16), axis=0, keepdims=True)
    for j in range(height):
        note[0, j : j + 1, :] = offset[:, j * lanes : (j + 1) * lanes]


def pair_kernel(kept, received, near, *rest):
    *outs, near_out = rest
    near_out[...] = near[...]
    span = outs[0].shape[0]
    for m, out in enumerate(outs):
        at = slice(m * span, (m + 1) * span)
        out[...] = (kept[at, :] + received[at, :].astype(f32)).astype(bf16)


def both_kernel(note, note_other, notes):
    notes[0] = note[0]
    notes[1] = note_other[0]


def finish_kernel(shards, many, widths, own, *rest):
    fars = shards // 2
    parts = rest[:fars]
    notes = rest[fars:-4]
    unit_out, turned = rest[-2:]
    span, width_out = own.shape
    height = width_out // lanes
    me = lax.axis_index("mp")
    width = jnp.where(lax.axis_index("group") == 0, widths[0], widths[1]).astype(f32)
    rows_of = []
    for n in notes:
        rows_of += [(n, i) for i in range(n.shape[0])]
    tail = notes[0].shape[1] - height
    stacked = [n[i, height:, :] for n, i in rows_of]
    stacked.append(jnp.zeros((-(-shards * tail // lanes) * lanes - shards * tail, lanes), f32))
    turned[...] = jnp.transpose(jnp.concatenate(stacked, axis=0))
    first = me * span
    block = turned[pl.ds(pl.multiple_of(lax.rem(first, lanes), span), span), :]
    lane = lax.broadcasted_iota(jnp.int32, block.shape, 1)
    pick = lax.div(first, lanes)

    def column(at):
        return jnp.sum(jnp.where(lane == at + pick, block, 0.0), axis=1, keepdims=True)

    means = [column(k * tail) for k in range(shards)]
    spreads = [column(k * tail + many) for k in range(shards)]
    mean = tree(means, jnp.add) / shards
    spread = tree(spreads, jnp.add) / width
    spread += tree([(m - mean) * (m - mean) for m in means], jnp.add) / shards
    inverse = lax.rsqrt(spread + norm_epsilon)
    pieces = []
    squares = jnp.zeros((span, lanes), f32)
    for j in range(height):
        at = slice(j * lanes, (j + 1) * lanes)
        value = own[:, at]
        for part in parts:
            value += part[:, at].astype(f32)
        for k, (n, i) in enumerate(rows_of):
            value += (means[k] - mean) * n[i, j : j + 1, :]
        value *= inverse
        squares += value * value
        pieces.append(value)
    scale = lax.rsqrt(jnp.sum(squares, axis=1, keepdims=True) + unit_epsilon)
    for j in range(height):
        unit_out[:, j * lanes : (j + 1) * lanes] = (pieces[j] * scale).astype(bf16)


def scores_kernel(halves, shards, multiplier, left, right, *rest):
    owns = rest[:4]
    others = rest[4:-4]
    scores_out, column_out, gathered, mine = rest[-4:]
    span = owns[0].shape[0]
    fars = shards // 2
    dp, mp = lax.axis_index("dp"), lax.axis_index("mp")
    core, near = lax.rem(dp, 2), lax.rem(mp, 2)
    half, far = lax.div(dp, 2), lax.div(mp, 2)
    for h in range(halves):
        for m in range(fars):
            at = ((half ^ h) * fars + (far ^ m)) * span
            gathered[pl.ds(pl.multiple_of(at, span), span), :] = others[h * fars + m][...]
    for c in range(2):
        for n in range(2):
            at = ((core ^ c) * 2 + (near ^ n)) * span
            mine[pl.ds(pl.multiple_of(at, span), span), :] = owns[c * 2 + n][...]
    scores = multiplier[0] * lax.dot_general(
        mine[...], gathered[...], (((1,), (1,)), ((), ())), preferred_element_type=f32
    )
    scores_out[...] = scores
    column_peak = jnp.max(scores, axis=0, keepdims=True)
    column_part = column_peak + jnp.log(
        jnp.sum(jnp.exp(scores - column_peak), axis=0, keepdims=True)
    )
    matched = left[...] == right[...]
    target = jnp.sum(jnp.where(matched, scores, 0.0), axis=0, keepdims=True)
    row = lax.broadcasted_iota(jnp.int32, column_out.shape, 0)
    column_out[...] = jnp.where(row == 0, column_part, jnp.where(row == 1, target, 0.0))


def rows_kernel(scores, out):
    values = scores[...]
    peak = jnp.max(values, axis=1, keepdims=True)
    part = peak + jnp.log(jnp.sum(jnp.exp(values - peak), axis=1, keepdims=True))
    out[...] = jnp.transpose(jnp.broadcast_to(part, (values.shape[0], lanes)))[0:1, :]


def merge_rows_kernel(row, row_other, out):
    out[...] = jnp.broadcast_to(log_add(row[...], row_other[...]), out.shape)


def merge_columns_kernel(column, column_other, after, out):
    out[...] = merge_columns(column[0:2, :], column_other[0:2, :])


def grads_kernel(
    multiplier, left, right, scores, gathered, column, column_other, *rest
):
    row, row_other, sent_out, loss_out, weights = rest
    rows, width_out = sent_out.shape[0], gathered.shape[1]
    core = lax.rem(lax.axis_index("dp"), 2)
    row_total = log_add(row[0:1, :], row_other[0:1, :])
    column_both = merge_columns(column[...], column_other[...])
    column_total = column_both[0:1, :]
    loss = jnp.sum(column_total - column_both[1:2, :], axis=1, keepdims=True)
    loss = jnp.broadcast_to(loss, loss_out.shape)
    loss_out[...] = loss
    sent_out[:, width_out:] = split_rows(loss, rows)
    row_total = jnp.transpose(jnp.broadcast_to(row_total, (lanes, row_total.shape[1])))[:, 0:1]
    matched = left[...] == right[...]
    values = scores[...]
    weights[...] = (
        multiplier[0]
        * (
            jnp.exp(values - row_total)
            + jnp.exp(values - column_total)
            - jnp.where(matched, 2.0, 0.0)
        )
    ).astype(bf16)
    part = weights[pl.ds(pl.multiple_of((1 - core) * rows, rows), rows), :]
    sent_out[:, :width_out] = jnp.dot(
        part, gathered[...], preferred_element_type=f32
    ).astype(bf16)


def kept_kernel(weights, gathered, out):
    rows = out.shape[0]
    core = lax.rem(lax.axis_index("dp"), 2)
    part = weights[pl.ds(pl.multiple_of(core * rows, rows), rows), :]
    out[...] = jnp.dot(part, gathered[...], preferred_element_type=f32)


def halve_kernel(kept, received, loss, own_out, sent_out, loss_out):
    rows, width_out = own_out.shape
    near = lax.rem(lax.axis_index("mp"), 2)
    mine = pl.ds(pl.multiple_of(near * rows, rows), rows)
    yours = pl.ds(pl.multiple_of((1 - near) * rows, rows), rows)
    loss = loss[...] + jnp.sum(received[:, width_out:].astype(f32), axis=0, keepdims=True)
    loss_out[...] = loss
    own_out[...] = kept[mine, :] + received[mine, :width_out].astype(f32)
    sent_out[:, :width_out] = (kept[yours, :] + received[yours, :width_out].astype(f32)).astype(bf16)
    sent_out[:, width_out:] = split_rows(loss, rows)


def body(
    image_features, text_features, image_gain, text_gain, image_proj, text_proj, pair, logit_scale
):
    rows = image_features.shape[0]
    shards = lax.axis_size("mp")
    owners = lax.axis_size("dp")
    halves, fars = owners // 2, shards // 2
    span = rows // shards
    width_out = image_proj.shape[1]
    group = lax.axis_index("group")
    me = lax.axis_index("mp")
    owner = lax.axis_index("dp")
    many = rows // lanes
    note_height = -(-(width_out // lanes + 2 * many) // 8) * 8
    shape = jax.ShapeDtypeStruct

    def project(x, gain, p):
        width = x.shape[1]
        return pl.pallas_call(
            functools.partial(project_kernel, shards),
            out_shape=[
                shape((span, width_out), f32),
                shape(((fars - 1) * span, width_out), f32),
                shape((span, width_out), bf16),
                shape(((fars - 1) * span, width_out), bf16),
                shape((1, note_height, lanes), f32),
            ],
            in_specs=[HBM, VMEM, HBM],
            out_specs=[VMEM] * 5,
            scratch_shapes=[
                pltpu.VMEM((rows, width), bf16),
                pltpu.VMEM((width, width_out), bf16),
                pltpu.VMEM((rows + 16, width), bf16),
                pltpu.VMEM((rows + 16, width_out), f32),
                pltpu.VMEM((rows, lanes), f32),
                pltpu.SemaphoreType.DMA((X_CUTS + max(1, width // P_STEP),)),
            ],
            compiler_params=PARAMS_P,
            name="project",
        )(x, gain, p)

    own, kept, near_part, far_part, note = lax.cond(
        group == 0,
        lambda: project(text_features, text_gain, text_proj),
        lambda: project(image_features, image_gain, image_proj),
    )
    far_other = exchange(far_part, "mp", 1)
    note_other = exchange(note, "mp", 1)
    *pairs, near_part = pl.pallas_call(
        pair_kernel,
        out_shape=[shape((span, width_out), bf16)] * fars,
        in_specs=[VMEM] * 3,
        out_specs=[VMEM] * fars,
        compiler_params=PARAMS,
        name="pair",
    )(kept, far_other, near_part)
    both = pl.pallas_call(
        both_kernel,
        out_shape=shape((2, note_height, lanes), f32),
        in_specs=[VMEM] * 2,
        out_specs=VMEM,
        compiler_params=PARAMS,
        name="both",
    )(note, note_other)
    parts = []
    notes = [both]
    for m in range(1, fars):
        parts.append(exchange(pairs[m - 1], "mp", 2 * m))
        notes.append(exchange(both, "mp", 2 * m))
    parts.append(exchange(near_part, "mp", 1))

    core, near = owner % 2, me % 2
    half, far = owner // 2, me // 2
    numbers = jnp.arange(owners * rows, dtype=jnp.int32)
    cut = (halves, 2, fars, 2, span)

    def of_rows(v):
        return lax.dynamic_slice(
            v.reshape(cut), (half, 0, far, 0, 0), (1, 2, 1, 2, span)
        ).reshape(4 * span, 1)

    def of_columns(v):
        return lax.dynamic_slice(
            v.reshape(cut), (0, core, 0, near, 0), (halves, 1, fars, 1, span)
        ).reshape(1, halves * fars * span)

    image_rows = group == 0
    left = of_rows(jnp.where(image_rows, pair, numbers))
    right = of_columns(jnp.where(image_rows, numbers, pair))
    row_count, column_count = 4 * span, halves * fars * span
    multiplier = logit_scale.reshape(1)

    unit = pl.pallas_call(
        functools.partial(
            finish_kernel,
            shards,
            many,
            (text_features.shape[1] * shards, image_features.shape[1] * shards),
        ),
        out_shape=shape((span, width_out), bf16),
        in_specs=[VMEM] * (1 + len(parts) + len(notes) + 2),
        out_specs=VMEM,
        scratch_shapes=[
            pltpu.VMEM(
                (
                    lanes,
                    -(-shards * (note_height - width_out // lanes) // lanes) * lanes,
                ),
                f32,
            )
        ],
        compiler_params=PARAMS,
        name="finish",
    )(own, *parts, *notes, left, right)

    others = [unit] + [exchange(unit, "mp", m * 2) for m in range(1, fars)]
    owns = [cross_exchange(unit, 0), cross_exchange(unit, 1)]
    blocks = list(others)
    for h in range(1, halves):
        blocks += [exchange(b, "dp", h * 2) for b in others]
    owns += [exchange(b, "dp", 1) for b in owns]

    scores, column_part, gathered = pl.pallas_call(
        functools.partial(scores_kernel, halves, shards),
        out_shape=[
            shape((row_count, column_count), f32),
            shape((COLUMN_COPIES, column_count), f32),
            shape((column_count, width_out), bf16),
        ],
        in_specs=[SMEM] + [VMEM] * (2 + 4 + halves * fars),
        out_specs=[VMEM] * 3,
        scratch_shapes=[pltpu.VMEM((row_count, width_out), bf16)],
        compiler_params=PARAMS,
        name="scores",
    )(multiplier, left, right, *owns, *blocks)

    def merged(kernel, height, *operands):
        return pl.pallas_call(
            kernel,
            out_shape=shape((height, operands[0].shape[1]), f32),
            in_specs=[VMEM] * len(operands),
            out_specs=VMEM,
            compiler_params=PARAMS,
            name="merge",
        )(*operands)

    row_part = pl.pallas_call(
        rows_kernel,
        out_shape=shape((1, row_count), f32),
        in_specs=[VMEM],
        out_specs=VMEM,
        compiler_params=PARAMS,
        name="rows",
    )(scores)

    column_steps = [("dp", 2 << i) for i in range((halves - 1).bit_length())]
    column_steps += [("mp", 2 << i) for i in range((fars - 1).bit_length())]
    row, column = row_part, column_part
    row = merged(merge_rows_kernel, ROW_COPIES, row, exchange(row, "dp", 1))
    row_other = exchange(row, "mp", 1)
    for axis, distance in column_steps[:-1]:
        column = merged(merge_columns_kernel, 2, column, exchange(column, axis, distance), row)
    column_other = exchange(column, *column_steps[-1])

    sent, loss, weights = pl.pallas_call(
        grads_kernel,
        out_shape=[
            shape((2 * span, width_out + lanes), bf16),
            shape((1, lanes), f32),
            shape((row_count, column_count), bf16),
        ],
        in_specs=[SMEM] + [VMEM] * 8,
        out_specs=[VMEM] * 3,
        compiler_params=PARAMS,
        name="grads",
    )(multiplier, left, right, scores, gathered, column, column_other, row, row_other)
    kept = pl.pallas_call(
        kept_kernel,
        out_shape=shape((2 * span, width_out), f32),
        in_specs=[VMEM] * 2,
        out_specs=VMEM,
        compiler_params=PARAMS,
        name="kept",
    )(weights, gathered)
    own, sent, loss = pl.pallas_call(
        halve_kernel,
        out_shape=[
            shape((span, width_out), f32),
            shape((span, width_out + lanes), bf16),
            shape((1, lanes), f32),
        ],
        in_specs=[VMEM] * 3,
        out_specs=[VMEM] * 3,
        compiler_params=PARAMS,
        name="halve",
    )(kept, exchange(sent, "dp", 1), loss)
    there, there_near = cross_exchange(loss, 0), cross_exchange(loss, 1)
    received = exchange(sent, "mp", 1)
    grads = own + received[:, :width_out].astype(f32)
    near_loss = jnp.sum(received[:, width_out:].astype(f32), axis=0, keepdims=True)
    loss = ((loss + near_loss) + (there + there_near)) * (1.0 / (2.0 * owners * rows))
    return (grads[None, :, :], loss[0, 0])


def solution(mesh):
    in_specs = (
        P("dp", "mp"),
        P("dp", "mp"),
        P("mp"),
        P("mp"),
        P("mp", None),
        P("mp", None),
        P(),
        P(),
    )
    out_specs = (P("group", ("dp", "mp"), None), P())
    return jax.shard_map(body, mesh=mesh, in_specs=in_specs, out_specs=out_specs, check_vma=False)
```
